32 devices in a mesh: grp: 1, res: 16 (over z, y, core), seq: 2 (over x).
Axes of the slice: x: 2, y: 2, z: 4, core: 2. Of those that a mesh axis runs over, the one named last changes fastest.
Arguments:
- alignment_activations: bfloat16 [16, 256, 64], P(('grp', 'seq'), 'res'), may hold values from -6 to 6
- alignment_row_mask: int32 [16], P(('grp', 'seq')), may hold values 0 or 1
- residue_mask: int32 [256], P('grp'), may hold values 0 or 1
- pair_head_logits: bfloat16 [8, 256, 256], P(None, ('grp', 'res')), may hold values from -300 to 300, as said below
- value_matrix: bfloat16 [64, 256], replicated, may hold values from -0.75 to 0.75
- gate_matrix: bfloat16 [64, 256], replicated, may hold values from -0.75 to 0.75
- output_matrix: bfloat16 [256, 64], replicated, may hold values from -0.375 to 0.375
- cotangent: bfloat16 [16, 256, 64], P(('grp', 'seq'), 'res'), may hold values from -6 to 6
Outputs:
- alignment_gradient: float32 [16, 256, 64], P(('grp', 'seq'), 'res')
- pair_logit_gradient: float32 [8, 256, 256], P(None, ('grp', 'res'), 'seq')
- value_weight_gradient: float32 [64, 256], P('grp')
- gate_weight_gradient: float32 [64, 256], P('grp')
- output_weight_gradient: float32 [256, 64], P('grp')
The draws below stay inside these ranges and needn't reach their ends.
Inputs may be any that keep to these rules, and one draw needn't show every extreme that they name: `pair_head_logits`: bfloat16 logits.
All inputs are finite; a program needn't handle non-finite values. No bound on the sum of `alignment_row_mask` on one device may be relied on, other than what follows from the above.
Results may differ from the reference program's by a relative error of at most 0.0071.
Values may be sent and summed in bfloat16 or wider, within the bound.
No kernel may reach another device: no remote copies, remote signals or barrier semaphores. Data moves between devices by JAX's collectives and lax.ppermute only.
A program may use at most 64 MiB of HBM per device.

```python
import jax
import jax.numpy as jnp
from jax import lax

ALIGNMENT_DEPTH = 64
HEADS = 8
HEAD_DIM = 32
VALUE_CHANNELS = 256
RESIDUE_COUNT = 256
ALIGNED_ROWS = 16


def draw_pair_head_logits(key, part):
    key = jax.random.fold_in(key, 7)
    keys = jax.random.split(key, 1)
    array_extent = (HEADS, RESIDUE_COUNT, RESIDUE_COUNT)
    result = jnp.clip(3.0 * jax.random.normal(keys[0], array_extent, jnp.float32), -12.0, 12.0)
    return result.astype(jnp.bfloat16)


def place_ends(drawn, key, low, largest):
    longest = drawn.shape.index(max(drawn.shape))
    spots = []
    for shift in (0, 1):
        where = [jax.random.randint(jax.random.fold_in(key, axis), (), 0, length) for axis, length in enumerate(drawn.shape)]
        where[longest] = (where[longest] + shift) % drawn.shape[longest]
        spots.append(tuple(where))
    return drawn.at[spots[0]].set(low).at[spots[1]].set(largest)


def block_levels(key, shape, cuts, low, top_value):
    loudness = 1.0
    for dim, parts in cuts:
        draws = jax.random.uniform(jax.random.fold_in(jax.random.fold_in(key, 6), dim), (parts,), jnp.float32, low / len(cuts), top_value / len(cuts))
        loudness = loudness * jnp.repeat(jnp.exp(draws), shape[dim] // parts).reshape((-1,) + (1,) * (len(shape) - 1 - dim))
    return loudness


def bell_draw(rng, extent, width, reach, shards=(), held_as=jnp.bfloat16):
    array = width * jax.random.normal(rng, extent, jnp.float32)
    if shards:
        array = array * block_levels(rng, extent, shards, -0.22, 0.18)
    return jnp.clip(array, -reach, reach).astype(held_as)


def setup_inputs(seed: int = 0, part: int = 0) -> dict:
    key_of = jax.random.split(jax.random.key(seed), 9)
    part_splits = jax.random.split(jax.random.fold_in(key_of[8], part), 9)
    alignment_activations = bell_draw(part_splits[0], (ALIGNED_ROWS, RESIDUE_COUNT, ALIGNMENT_DEPTH), 1.0, 6.0, ((0, 2), (1, 16)))
    alignment_row_mask = place_ends((jax.random.randint(part_splits[1], (ALIGNED_ROWS,), 0, 4) < 3).astype(jnp.int32), jax.random.fold_in(part_splits[1], 1), 0, 1)
    residue_mask = place_ends((jax.random.randint(part_splits[2], (RESIDUE_COUNT,), 0, 8) < 7).astype(jnp.int32), jax.random.fold_in(part_splits[2], 1), 0, 1)
    pair_head_logits = draw_pair_head_logits(jax.random.fold_in(jax.random.fold_in(key_of[8], part), 71), part)
    value_matrix = bell_draw(key_of[4], (ALIGNMENT_DEPTH, VALUE_CHANNELS), ALIGNMENT_DEPTH ** -0.5, 0.75)
    gate_matrix = bell_draw(key_of[5], (ALIGNMENT_DEPTH, VALUE_CHANNELS), ALIGNMENT_DEPTH ** -0.5, 0.75)
    output_matrix = bell_draw(key_of[6], (VALUE_CHANNELS, ALIGNMENT_DEPTH), VALUE_CHANNELS ** -0.5, 0.375)
    cotangent = bell_draw(part_splits[7], (ALIGNED_ROWS, RESIDUE_COUNT, ALIGNMENT_DEPTH), 1.0, 6.0, ((0, 2), (1, 16)))
    return {"alignment_activations": alignment_activations, "alignment_row_mask": alignment_row_mask, "residue_mask": residue_mask, "pair_head_logits": pair_head_logits, "value_matrix": value_matrix, "gate_matrix": gate_matrix, "output_matrix": output_matrix, "cotangent": cotangent}


def layer_standardize(alignment_activations):
    activation_input = alignment_activations.astype(jnp.float32)
    mean_val = lax.optimization_barrier(jnp.mean(activation_input, axis=-1, keepdims=True))
    centered = activation_input - mean_val
    variance = lax.optimization_barrier(jnp.mean(centered * centered, axis=-1, keepdims=True))
    inverse_deviation = lax.rsqrt(variance + 1e-05)
    return (centered * inverse_deviation, inverse_deviation)

def reference(alignment_activations, alignment_row_mask, residue_mask, pair_head_logits, value_matrix, gate_matrix, output_matrix, cotangent):
    unit_alignment, inverse_deviation = layer_standardize(alignment_activations)
    standardized_rows = unit_alignment.astype(jnp.bfloat16)
    values = jnp.dot(standardized_rows, value_matrix, preferred_element_type=jnp.float32).astype(jnp.bfloat16)
    gate_act = jax.nn.sigmoid(jnp.dot(standardized_rows, gate_matrix, preferred_element_type=jnp.float32))
    key_live = residue_mask == 1
    scores = jnp.where(key_live[None, None, :], pair_head_logits.astype(jnp.float32), -10000.0)
    prob_full = jax.nn.softmax(scores, axis=-1)
    weights = prob_full.astype(jnp.bfloat16)
    row_keep = alignment_row_mask.astype(jnp.float32)[:, None, None]
    values_heads = values.astype(jnp.float32).reshape(ALIGNED_ROWS, RESIDUE_COUNT, HEADS, HEAD_DIM)
    weights_wide = weights.astype(jnp.float32)
    attended = jnp.einsum('hij,sjhc->sihc', weights_wide, values_heads).reshape(ALIGNED_ROWS, RESIDUE_COUNT, VALUE_CHANNELS)
    mixed_out = (gate_act * attended * row_keep).astype(jnp.bfloat16)
    grad_mixed = lax.dot_general(cotangent, output_matrix, (((2,), (1,)), ((), ())), preferred_element_type=jnp.float32)
    grad_att = (grad_mixed * gate_act * row_keep).astype(jnp.bfloat16)
    gate_grad = (grad_mixed * attended * row_keep * gate_act * (1.0 - gate_act)).astype(jnp.bfloat16)
    output_weight_gradient = jnp.einsum('sic,sid->cd', mixed_out.astype(jnp.float32), cotangent.astype(jnp.float32))
    att_heads = grad_att.astype(jnp.float32).reshape(ALIGNED_ROWS, RESIDUE_COUNT, HEADS, HEAD_DIM)
    grad_prob = jnp.einsum('sihc,sjhc->hij', att_heads, values_heads)
    pair_logit_gradient = prob_full * (grad_prob - lax.optimization_barrier(jnp.sum(prob_full * grad_prob, axis=-1, keepdims=True)))
    grad_values = jnp.einsum('hij,sihc->sjhc', weights_wide, att_heads).reshape(ALIGNED_ROWS, RESIDUE_COUNT, VALUE_CHANNELS).astype(jnp.bfloat16)
    gradient_standardized = jnp.dot(grad_values, value_matrix.T, preferred_element_type=jnp.float32)
    gradient_standardized = gradient_standardized + jnp.dot(gate_grad, gate_matrix.T, preferred_element_type=jnp.float32)
    normed_wide = standardized_rows.astype(jnp.float32)
    value_weight_gradient = jnp.einsum('sic,sid->cd', normed_wide, grad_values.astype(jnp.float32))
    gate_weight_gradient = jnp.einsum('sic,sid->cd', normed_wide, gate_grad.astype(jnp.float32))
    leading_average = lax.optimization_barrier(jnp.mean(gradient_standardized, axis=-1, keepdims=True))
    trailing_average = lax.optimization_barrier(jnp.mean(gradient_standardized * unit_alignment, axis=-1, keepdims=True))
    alignment_gradient = inverse_deviation * (gradient_standardized - leading_average - unit_alignment * trailing_average)
    return (alignment_gradient, pair_logit_gradient, value_weight_gradient, gate_weight_gradient, output_weight_gradient)
```

```python
import functools

import jax
import jax.numpy as jnp
from jax import lax
from jax.experimental import pallas as pl
from jax.experimental.pallas import tpu as pltpu
from jax.sharding import PartitionSpec as P

LANES = 128
F32 = jnp.float32
BF16 = jnp.bfloat16


def dot(a, b):
    return lax.dot_general(a, b, (((1,), (0,)), ((), ())), preferred_element_type=F32)


def dot_nt(a, b):
    return lax.dot_general(a, b, (((1,), (1,)), ((), ())), preferred_element_type=F32)


def dot_tn(a, b):
    return lax.dot_general(a, b, (((0,), (0,)), ((), ())), preferred_element_type=F32)


def standardize(x):
    x = x.astype(F32)
    centered = x - jnp.mean(x, axis=-1, keepdims=True)
    inv = lax.rsqrt(jnp.mean(centered * centered, axis=-1, keepdims=True) + 1e-05)
    return centered * inv, inv


def pack_kernel(acts_ref, cot_ref, logits_ref, live_ref, pack_ref, prob_ref):
    rows, own, depth = acts_ref.shape
    heads, _, keys = logits_ref.shape
    unit, _ = standardize(acts_ref[...])
    normed = unit.astype(BF16)
    cot = cot_ref[...]
    per = LANES // depth
    blocks = rows // per
    for b in range(blocks):
        pack_ref[pl.ds(b * own, own), :] = jnp.concatenate(
            [normed[b * per + k] for k in range(per)], axis=-1
        )
        pack_ref[pl.ds((blocks + b) * own, own), :] = jnp.concatenate(
            [cot[b * per + k] for k in range(per)], axis=-1
        )
    live = live_ref[...] == 1
    wide = keys // LANES
    for h in range(heads):
        scores = jnp.where(live, logits_ref[h].astype(F32), -10000.0)
        e = jnp.exp(scores - jnp.max(scores, axis=-1, keepdims=True))
        prob = e / jnp.sum(e, axis=-1, keepdims=True)
        prob_ref[h] = prob
        weights = prob.astype(BF16)
        for w in range(wide):
            pack_ref[pl.ds((2 * blocks + h * wide + w) * own, own), :] = weights[
                :, w * LANES : (w + 1) * LANES
            ]


def main_kernel(
    heads,
    where_ref,
    keep_ref,
    acts_ref,
    prob_ref,
    all_ref,
    value_ref,
    gate_ref,
    output_ref,
    align_ref,
    pair_own_ref,
    pair_send_ref,
    totals_ref,
    att_ref,
    val_grad_ref,
    gate_grad_ref,
):
    rows, own, depth = acts_ref.shape
    parts, _, _, _ = all_ref.shape
    keys = parts * own
    width = value_ref.shape[1]
    dim = width // heads
    quad = LANES // dim
    groups = rows // quad
    per = LANES // depth
    blocks = rows // per
    wide = keys // LANES
    first = pl.multiple_of(where_ref[0] * own, own)
    half = where_ref[1]

    def lane_block(k):
        return all_ref[:, k].reshape(keys, LANES)

    span = quad // per
    x = [
        jnp.concatenate([lane_block(g * span + k) for k in range(span)], axis=1)
        for g in range(groups)
    ]
    y = [
        jnp.concatenate([lane_block(blocks + g * span + k) for k in range(span)], axis=1)
        for g in range(groups)
    ]
    x_t = [a.T for a in x]
    y_t = [a.T for a in y]

    lane = lax.broadcasted_iota(jnp.int32, (1, LANES), 1)
    slot = lane // dim
    keep = []
    for g in range(groups):
        row = jnp.zeros((1, LANES), F32)
        for k in range(quad):
            row = jnp.where(slot == k, keep_ref[g * quad + k].astype(F32), row)
        keep.append(row)
    keep_row = jnp.concatenate(keep, axis=1)

    src = lax.broadcasted_iota(jnp.int32, (width, 2 * LANES), 0)
    dst = lax.broadcasted_iota(jnp.int32, (width, 2 * LANES), 1)
    dst_slot = (dst % LANES) // dim
    spread_to = (dst // LANES) * dim + dst % dim
    mask_row = lax.broadcasted_iota(jnp.int32, (quad * depth, 2 * LANES), 0) // depth
    mask_col = (lax.broadcasted_iota(jnp.int32, (quad * depth, 2 * LANES), 1) % LANES) // dim
    diagonal = mask_row == mask_col
    fold_slot = dst_slot[:depth]

    def block_diagonal(ref, p):
        spread = (src == spread_to + 2 * p * dim).astype(BF16)
        wide_rows = dot(ref[...], spread)
        tall = jnp.concatenate([wide_rows] * quad, axis=0)
        return jnp.where(diagonal, tall, 0.0).astype(BF16)

    def fold(total):
        picked = total[:depth]
        for k in range(1, quad):
            picked = jnp.where(fold_slot == k, total[k * depth : (k + 1) * depth], picked)
        out = []
        for h in range(2):
            part = picked[:, h * LANES : (h + 1) * LANES]
            step = LANES // 2
            while step >= dim:
                part = part + pltpu.roll(part, step, 1)
                step //= 2
            out.append(part)
        return out

    folded = [[], [], []]
    grad_normed = [jnp.zeros((own, quad * depth), F32) for _ in range(groups)]
    sums = jnp.zeros((own, LANES), F32)
    for p in range(heads // 2):
        value_bd = block_diagonal(value_ref, p)
        gate_bd = block_diagonal(gate_ref, p)
        output_bd = block_diagonal(output_ref, p)
        values = [dot(a, value_bd).astype(BF16) for a in x]
        gates = [dot(a, gate_bd) for a in x]
        mixes = [dot(a, output_bd) for a in y]
        mixed_out, gate_grad, val_grad = [], [], []
        for k in range(2):
            h = 2 * p + k
            cut = slice(k * LANES, (k + 1) * LANES)
            weights = jnp.concatenate(
                [lane_block(2 * blocks + h * wide + w) for w in range(wide)], axis=1
            )
            vals = jnp.concatenate([v[:, cut] for v in values], axis=1)
            attended = dot(weights, vals)
            gate = jax.nn.sigmoid(jnp.concatenate([v[:, cut] for v in gates], axis=1))
            mixed = jnp.concatenate([v[:, cut] for v in mixes], axis=1)
            kept = gate * keep_row
            grad_att = mixed * kept
            att_bf = grad_att.astype(BF16)
            att_ref[h] = att_bf
            mixed_out.append((kept * attended).astype(BF16))
            gate_grad.append((grad_att * attended * (1.0 - gate)).astype(BF16))
            val_grad.append(dot_tn(weights, att_bf).astype(BF16))
            pair = dot_nt(att_ref[h, pl.ds(first, own), :], vals)
            prob = prob_ref[h]
            sums = jnp.where(lane == h, jnp.sum(prob * pair, axis=-1, keepdims=True), sums)
            low, high = pair[:, : keys // 2], pair[:, keys // 2 :]
            pair_own_ref[h] = jnp.where(half == 0, low, high)
            pair_send_ref[h] = jnp.where(half == 0, high, low)
        totals = [None, None, None]
        for g in range(groups):
            cut = slice(g * LANES, (g + 1) * LANES)
            mo = jnp.concatenate([a[:, cut] for a in mixed_out], axis=1)
            gg = jnp.concatenate([a[:, cut] for a in gate_grad], axis=1)
            vg = jnp.concatenate([a[:, cut] for a in val_grad], axis=1)
            gate_grad_ref[p * groups + g] = gg
            val_grad_ref[p * groups + g] = vg
            grad_normed[g] = (
                grad_normed[g]
                + dot_nt(val_grad_ref[p * groups + g, pl.ds(first, own), :], value_bd)
                + dot_nt(gate_grad_ref[p * groups + g, pl.ds(first, own), :], gate_bd)
            )
            for t, (left, right) in enumerate(((x_t, vg), (x_t, gg), (y_t, mo))):
                term = dot(left[g], right)
                totals[t] = term if totals[t] is None else totals[t] + term
        for t in range(3):
            folded[t].extend(fold(totals[t]))

    pair_send_ref[heads] = sums
    pair_own_ref[heads] = sums
    for t in range(3):
        cols = []
        for b in range(width // LANES):
            block = folded[t][b * quad]
            for k in range(1, quad):
                block = jnp.where(slot == k, folded[t][b * quad + k], block)
            cols.append(block)
        totals_ref[pl.ds(t * depth, depth), :] = jnp.concatenate(cols, axis=1).astype(BF16)

    unit, inv = standardize(acts_ref[...])
    for s in range(rows):
        g, k = divmod(s, quad)
        grad = grad_normed[g][:, k * depth : (k + 1) * depth]
        lead = jnp.mean(grad, axis=-1, keepdims=True)
        trail = jnp.mean(grad * unit[s], axis=-1, keepdims=True)
        align_ref[s] = inv[s] * (grad - lead - unit[s] * trail)


def last_kernel(
    where_ref, prob_ref, own_ref, got_ref, totals_ref, more_ref, pair_ref, value_ref, gate_ref, output_ref
):
    heads = prob_ref.shape[0]
    share = own_ref.shape[2]
    half = where_ref[1]
    sums = own_ref[heads] + got_ref[heads]
    for h in range(heads):
        prob = jnp.where(half == 0, prob_ref[h, :, :share], prob_ref[h, :, share:])
        pair_ref[h] = prob * (own_ref[h] + got_ref[h] - sums[:, h : h + 1])
    depth = value_ref.shape[0]
    for t, ref in enumerate((value_ref, gate_ref, output_ref)):
        rows = pl.ds(t * depth, depth)
        ref[...] = totals_ref[rows, :].astype(F32) + more_ref[rows, :].astype(F32)


def call(kernel, outs, spaces, scratch=()):
    spec = {
        "v": pl.BlockSpec(memory_space=pltpu.VMEM),
        "s": pl.BlockSpec(memory_space=pltpu.SMEM),
    }
    return pl.pallas_call(
        kernel,
        out_shape=[jax.ShapeDtypeStruct(s, d) for s, d in outs],
        in_specs=[spec[c] for c in spaces],
        out_specs=[spec["v"]] * len(outs),
        scratch_shapes=list(scratch),
        compiler_params=pltpu.CompilerParams(vmem_limit_bytes=48 * 1024 * 1024),
    )


def local_gathered(
    alignment_activations,
    alignment_row_mask,
    residue_mask,
    pair_head_logits,
    value_matrix,
    gate_matrix,
    output_matrix,
    cotangent,
):
    rows, own, depth = alignment_activations.shape
    heads, _, keys = pair_head_logits.shape
    width = value_matrix.shape[1]
    parts = keys // own
    lanes = (2 * rows * depth + heads * keys) // LANES
    where = jnp.stack([lax.axis_index("res"), lax.axis_index("seq")]).astype(jnp.int32)
    packed, prob = call(
        pack_kernel, [((lanes * own, LANES), BF16), ((heads, own, keys), F32)], "vvvv"
    )(alignment_activations, cotangent, pair_head_logits, residue_mask.reshape(1, keys))
    gathered = lax.all_gather(packed, "res", axis=0, tiled=True)
    gathered = gathered.reshape(parts, lanes, own, LANES)
    share = keys // 2
    align, pair_own, pair_send, totals = call(
        functools.partial(main_kernel, heads),
        [
            ((rows, own, depth), F32),
            ((heads + 1, own, share), F32),
            ((heads + 1, own, share), F32),
            ((3 * depth, width), BF16),
        ],
        "ssvvvvvv",
        [pltpu.VMEM((heads, keys, 2 * LANES), BF16)] * 3,
    )(
        where,
        alignment_row_mask,
        alignment_activations,
        prob,
        gathered,
        value_matrix,
        gate_matrix,
        output_matrix.T,
    )
    swap = [(0, 1), (1, 0)]
    pair_got = lax.ppermute(pair_send, "seq", swap)
    totals_got = lax.ppermute(totals, "seq", swap)
    pair, value_total, gate_total, output_total = call(
        last_kernel,
        [((heads, own, share), F32)] + [((depth, width), F32)] * 3,
        "svvvvv",
    )(where, prob, pair_own, pair_got, totals, totals_got)
    return align, pair, value_total, gate_total, output_total.T


def fits(mesh, rows, own, depth, heads, keys, width):
    dim = width // heads
    return (
        mesh.shape["seq"] == 2
        and keys == 2 * LANES
        and own % 16 == 0
        and depth == 2 * dim
        and dim == LANES // 4
        and heads % 4 == 0
        and rows == 8
    )


def layer_standardize(alignment_activations):
    activation_input = alignment_activations.astype(jnp.float32)
    mean_val = jnp.mean(activation_input, axis=-1, keepdims=True)
    centered = activation_input - mean_val
    variance = jnp.mean(centered * centered, axis=-1, keepdims=True)
    inverse_deviation = lax.rsqrt(variance + 1e-05)
    return (centered * inverse_deviation, inverse_deviation)


def gated_back(cot_rows, gate_act, row_keep, output_matrix):
    grad_mixed = lax.dot_general(
        cot_rows, output_matrix, (((2,), (1,)), ((), ())), preferred_element_type=jnp.float32
    )
    return (grad_mixed, (grad_mixed * gate_act * row_keep).astype(jnp.bfloat16))


def block_terms(
    weights, columns, values_all, gate_act, grad_mixed, grad_att, att_all, row_keep, head_count
):
    row_count, key_count, width = values_all.shape
    head_dim = width // head_count
    values_heads = values_all.reshape(row_count, key_count, head_count, head_dim)
    attended = jnp.einsum(
        "hij,sjhc->sihc", weights, values_heads, preferred_element_type=jnp.float32
    )
    attended = attended.reshape(row_count, -1, width)
    mixed_out = (gate_act * attended * row_keep).astype(jnp.bfloat16)
    gate_grad = (grad_mixed * attended * row_keep * gate_act * (1.0 - gate_act)).astype(
        jnp.bfloat16
    )
    att_heads = grad_att.reshape(row_count, -1, head_count, head_dim)
    pair_total = jnp.einsum(
        "sihc,sjhc->hij", att_heads, values_heads, preferred_element_type=jnp.float32
    )
    all_heads = att_all.reshape(row_count, key_count, head_count, head_dim)
    grad_values = jnp.einsum(
        "hij,sihc->sjhc", columns, all_heads, preferred_element_type=jnp.float32
    )
    grad_values = grad_values.reshape(row_count, -1, width).astype(jnp.bfloat16)
    return (pair_total, mixed_out, gate_grad, grad_values)


def local(
    alignment_activations,
    alignment_row_mask,
    residue_mask,
    pair_head_logits,
    value_matrix,
    gate_matrix,
    output_matrix,
    cotangent,
):
    head_count = pair_head_logits.shape[0]
    key_count = pair_head_logits.shape[2]
    unit_alignment, inverse_deviation = layer_standardize(alignment_activations)
    standardized_rows = unit_alignment.astype(jnp.bfloat16)
    key_live = residue_mask == 1
    scores = jnp.where(key_live[None, None, :], pair_head_logits.astype(jnp.float32), -10000.0)
    prob_full = jax.nn.softmax(scores, axis=-1)
    weights = prob_full.astype(jnp.bfloat16)
    columns = lax.all_to_all(weights, "res", split_axis=2, concat_axis=1, tiled=True)
    row_keep = alignment_row_mask.astype(jnp.float32)[:, None, None]
    gate_own = jax.nn.sigmoid(
        jnp.dot(standardized_rows, gate_matrix, preferred_element_type=jnp.float32)
    )
    mixed_own, att_own = gated_back(cotangent, gate_own, row_keep, output_matrix)
    normed_all, cot_all = (
        lax.all_gather(standardized_rows, "res", axis=1, tiled=True),
        lax.all_gather(cotangent, "res", axis=1, tiled=True),
    )
    values_all = jnp.dot(normed_all, value_matrix, preferred_element_type=jnp.float32).astype(
        jnp.bfloat16
    )
    gate_all = jax.nn.sigmoid(jnp.dot(normed_all, gate_matrix, preferred_element_type=jnp.float32))
    mixed_all, att_all = gated_back(cot_all, gate_all, row_keep, output_matrix)
    pair_total, mixed_out, gate_grad, grad_values = block_terms(
        weights, columns, values_all, gate_own, mixed_own, att_own, att_all, row_keep, head_count
    )
    output_weight_gradient = jnp.einsum(
        "sic,sid->cd", mixed_out, cotangent, preferred_element_type=jnp.float32
    )
    value_weight_gradient = jnp.einsum(
        "sic,sid->cd", standardized_rows, grad_values, preferred_element_type=jnp.float32
    )
    gate_weight_gradient = jnp.einsum(
        "sic,sid->cd", standardized_rows, gate_grad, preferred_element_type=jnp.float32
    )
    gradient_totals = lax.psum(
        (value_weight_gradient, gate_weight_gradient, output_weight_gradient), ("res", "seq")
    )
    gradient_standardized = jnp.dot(grad_values, value_matrix.T, preferred_element_type=jnp.float32)
    gradient_standardized = gradient_standardized + jnp.dot(
        gate_grad, gate_matrix.T, preferred_element_type=jnp.float32
    )
    leading_average = jnp.mean(gradient_standardized, axis=-1, keepdims=True)
    trailing_average = jnp.mean(gradient_standardized * unit_alignment, axis=-1, keepdims=True)
    alignment_gradient = inverse_deviation * (
        gradient_standardized - leading_average - unit_alignment * trailing_average
    )
    grad_prob = lax.psum(pair_total, "seq")
    full_grads = prob_full * (grad_prob - jnp.sum(prob_full * grad_prob, axis=-1, keepdims=True))
    share_width = key_count // lax.axis_size("seq")
    pair_logit_gradient = lax.dynamic_slice_in_dim(
        full_grads, lax.axis_index("seq") * share_width, share_width, 2
    )
    return (
        alignment_gradient,
        pair_logit_gradient,
        gradient_totals[0],
        gradient_totals[1],
        gradient_totals[2],
    )


def pick(mesh, *arrays):
    rows, own, depth = arrays[0].shape
    heads, _, keys = arrays[3].shape
    width = arrays[4].shape[1]
    if fits(mesh, rows, own, depth, heads, keys, width):
        return local_gathered(*arrays)
    return local(*arrays)


def solution(mesh):
    return jax.shard_map(
        functools.partial(pick, mesh),
        mesh=mesh,
        in_specs=(
            P(("grp", "seq"), "res", None),
            P(("grp", "seq")),
            P("grp"),
            P(None, ("grp", "res"), None),
            P(),
            P(),
            P(),
            P(("grp", "seq"), "res", None),
        ),
        out_specs=(
            P(("grp", "seq"), "res", None),
            P(None, ("grp", "res"), "seq"),
            P("grp", None),
            P("grp", None),
            P("grp", None),
        ),
        check_vma=False,
    )
```

```python
import functools

import jax
import jax.numpy as jnp
from jax import lax
from jax.experimental import pallas as pl
from jax.experimental.pallas import tpu as pltpu
from jax.sharding import PartitionSpec as P

LANES = 128
F32 = jnp.float32
BF16 = jnp.bfloat16


def dot(a, b):
    return lax.dot_general(a, b, (((1,), (0,)), ((), ())), preferred_element_type=F32)


def dot_nt(a, b):
    return lax.dot_general(a, b, (((1,), (1,)), ((), ())), preferred_element_type=F32)


def dot_tn(a, b):
    return lax.dot_general(a, b, (((0,), (0,)), ((), ())), preferred_element_type=F32)


def standardize(x):
    x = x.astype(F32)
    centered = x - jnp.mean(x, axis=-1, keepdims=True)
    inv = lax.rsqrt(jnp.mean(centered * centered, axis=-1, keepdims=True) + 1e-05)
    return centered * inv, inv


def fetch(sources, targets, sems):
    copies = [
        pltpu.make_async_copy(src, dst, sems.at[i])
        for i, (src, dst) in enumerate(zip(sources, targets))
    ]
    for copy in copies:
        copy.start()
    return copies


def pack_kernel(
    acts_hbm, cot_hbm, logits_hbm, live_hbm, pack_ref, prob_ref,
    acts_ref, cot_ref, logits_ref, live_ref, sems,
):
    copies = fetch(
        (acts_hbm, cot_hbm, logits_hbm, live_hbm), (acts_ref, cot_ref, logits_ref, live_ref), sems
    )
    rows, own, depth = acts_ref.shape
    heads, _, keys = logits_ref.shape
    per = LANES // depth
    blocks = rows // per
    wide = keys // LANES
    copies[0].wait()
    unit, _ = standardize(acts_ref[...])
    normed = unit.astype(BF16)
    for b in range(blocks):
        pack_ref[pl.ds(b * own, own), :] = jnp.concatenate(
            [normed[b * per + k] for k in range(per)], axis=-1
        )
    copies[1].wait()
    cot = cot_ref[...]
    for b in range(blocks):
        pack_ref[pl.ds((blocks + b) * own, own), :] = jnp.concatenate(
            [cot[b * per + k] for k in range(per)], axis=-1
        )
    copies[2].wait()
    copies[3].wait()
    live = live_ref[...] == 1
    for h in range(heads):
        scores = jnp.where(live, logits_ref[h].astype(F32), -10000.0)
        e = jnp.exp(scores - jnp.max(scores, axis=-1, keepdims=True))
        prob = e / jnp.sum(e, axis=-1, keepdims=True)
        prob_ref[h] = prob
        weights = prob.astype(BF16)
        for w in range(wide):
            pack_ref[pl.ds((2 * blocks + h * wide + w) * own, own), :] = weights[
                :, w * LANES : (w + 1) * LANES
            ]


def prepare_kernel(
    heads,
    keep_ref,
    acts_ref,
    value_ref,
    gate_ref,
    output_ref,
    spread_ref,
    keep_row_ref,
    unit_ref,
    inv_ref,
):
    rows, _, depth = acts_ref.shape
    width = value_ref.shape[1]
    dim = width // heads
    quad = LANES // dim
    slot = lax.broadcasted_iota(jnp.int32, (1, LANES), 1) // dim
    for g in range(rows // quad):
        row = jnp.zeros((1, LANES), F32)
        for k in range(quad):
            row = jnp.where(slot == k, keep_ref[g * quad + k].astype(F32), row)
        keep_row_ref[:, g * LANES : (g + 1) * LANES] = row
    src = lax.broadcasted_iota(jnp.int32, (width, 2 * LANES), 0)
    dst = lax.broadcasted_iota(jnp.int32, (width, 2 * LANES), 1)
    spread_to = (dst // LANES) * dim + dst % dim
    mask_row = lax.broadcasted_iota(jnp.int32, (quad * depth, 2 * LANES), 0) // depth
    mask_col = (lax.broadcasted_iota(jnp.int32, (quad * depth, 2 * LANES), 1) % LANES) // dim
    diagonal = mask_row == mask_col
    for p in range(heads // 2):
        spread = (src == spread_to + 2 * p * dim).astype(BF16)
        for t, ref in enumerate((value_ref, gate_ref, output_ref)):
            tall = jnp.concatenate([dot(ref[...], spread)] * quad, axis=0)
            spread_ref[t, p] = jnp.where(diagonal, tall, 0.0).astype(BF16)
    unit, inv = standardize(acts_ref[...])
    unit_ref[...] = unit
    inv_ref[...] = jnp.broadcast_to(inv, unit.shape)


def main_kernel(
    heads,
    where_ref,
    prob_ref,
    near_ref,
    far_ref,
    spread_ref,
    keep_row_ref,
    unit_ref,
    inv_ref,
    align_ref,
    pair_own_ref,
    pair_send_ref,
    totals_ref,
    all_ref,
    att_ref,
    val_grad_ref,
    gate_grad_ref,
):
    rows, own, depth = unit_ref.shape
    parts, _, _, _ = all_ref.shape
    keys = parts * own
    dim = keep_row_ref.shape[1] // rows
    width = heads * dim
    quad = LANES // dim
    groups = rows // quad
    per = LANES // depth
    blocks = rows // per
    wide = keys // LANES
    first = pl.multiple_of(where_ref[0] * own, own)
    half = where_ref[1]
    for r in range(parts):
        away = where_ref[0] ^ r
        spot = (away // 2 % 2) * (parts // 4) + away // 4
        all_ref[r] = jnp.where(away % 2 == 0, near_ref[spot], far_ref[spot])

    def lane_block(k):
        return all_ref[:, k].reshape(keys, LANES)

    span = quad // per
    x = [
        jnp.concatenate([lane_block(g * span + k) for k in range(span)], axis=1)
        for g in range(groups)
    ]
    y = [
        jnp.concatenate([lane_block(blocks + g * span + k) for k in range(span)], axis=1)
        for g in range(groups)
    ]
    x_t = [a.T for a in x]
    y_t = [a.T for a in y]

    lane = lax.broadcasted_iota(jnp.int32, (1, LANES), 1)
    slot = lane // dim
    keep_row = keep_row_ref[...]
    fold_slot = (lax.broadcasted_iota(jnp.int32, (depth, 2 * LANES), 1) % LANES) // dim

    def fold(total):
        picked = total[:depth]
        for k in range(1, quad):
            picked = jnp.where(fold_slot == k, total[k * depth : (k + 1) * depth], picked)
        out = []
        for h in range(2):
            part = picked[:, h * LANES : (h + 1) * LANES]
            step = LANES // 2
            while step >= dim:
                part = part + pltpu.roll(part, step, 1)
                step //= 2
            out.append(part)
        return out

    folded = [[], [], []]
    grad_normed = [jnp.zeros((own, quad * depth), F32) for _ in range(groups)]
    sums = jnp.zeros((own, LANES), F32)
    for p in range(heads // 2):
        value_bd = spread_ref[0, p]
        gate_bd = spread_ref[1, p]
        output_bd = spread_ref[2, p]
        values = [dot(a, value_bd).astype(BF16) for a in x]
        gates = [dot(a, gate_bd) for a in x]
        mixes = [dot(a, output_bd) for a in y]
        mixed_out, gate_grad, val_grad = [], [], []
        for k in range(2):
            h = 2 * p + k
            cut = slice(k * LANES, (k + 1) * LANES)
            weights = jnp.concatenate(
                [lane_block(2 * blocks + h * wide + w) for w in range(wide)], axis=1
            )
            vals = jnp.concatenate([v[:, cut] for v in values], axis=1)
            attended = dot(weights, vals)
            gate = jax.nn.sigmoid(jnp.concatenate([v[:, cut] for v in gates], axis=1))
            mixed = jnp.concatenate([v[:, cut] for v in mixes], axis=1)
            kept = gate * keep_row
            grad_att = mixed * kept
            att_bf = grad_att.astype(BF16)
            att_ref[h] = att_bf
            mixed_out.append((kept * attended).astype(BF16))
            gate_grad.append((grad_att * attended * (1.0 - gate)).astype(BF16))
            val_grad.append(dot_tn(weights, att_bf).astype(BF16))
            pair = dot_nt(att_ref[h, pl.ds(first, own), :], vals)
            prob = prob_ref[h]
            sums = jnp.where(lane == h, jnp.sum(prob * pair, axis=-1, keepdims=True), sums)
            low, high = pair[:, : keys // 2], pair[:, keys // 2 :]
            pair_own_ref[h] = jnp.where(half == 0, low, high)
            pair_send_ref[h] = jnp.where(half == 0, high, low)
        totals = [None, None, None]
        for g in range(groups):
            cut = slice(g * LANES, (g + 1) * LANES)
            mo = jnp.concatenate([a[:, cut] for a in mixed_out], axis=1)
            gg = jnp.concatenate([a[:, cut] for a in gate_grad], axis=1)
            vg = jnp.concatenate([a[:, cut] for a in val_grad], axis=1)
            gate_grad_ref[p * groups + g] = gg
            val_grad_ref[p * groups + g] = vg
            grad_normed[g] = (
                grad_normed[g]
                + dot_nt(val_grad_ref[p * groups + g, pl.ds(first, own), :], value_bd)
                + dot_nt(gate_grad_ref[p * groups + g, pl.ds(first, own), :], gate_bd)
            )
            for t, (left, right) in enumerate(((x_t, vg), (x_t, gg), (y_t, mo))):
                term = dot(left[g], right)
                totals[t] = term if totals[t] is None else totals[t] + term
        for t in range(3):
            folded[t].extend(fold(totals[t]))

    pair_send_ref[heads] = sums
    pair_own_ref[heads] = sums
    for t in range(3):
        cols = []
        for b in range(width // LANES):
            block = folded[t][b * quad]
            for k in range(1, quad):
                block = jnp.where(slot == k, folded[t][b * quad + k], block)
            cols.append(block)
        totals_ref[pl.ds(t * depth, depth), :] = jnp.concatenate(cols, axis=1).astype(BF16)

    for s in range(rows):
        g, k = divmod(s, quad)
        grad = grad_normed[g][:, k * depth : (k + 1) * depth]
        lead = jnp.mean(grad, axis=-1, keepdims=True)
        trail = jnp.mean(grad * unit_ref[s], axis=-1, keepdims=True)
        align_ref[s] = inv_ref[s] * (grad - lead - unit_ref[s] * trail)


def last_kernel(
    where_ref, prob_ref, own_ref, got_ref, totals_ref, more_ref, pair_ref, value_ref, gate_ref, output_ref
):
    heads = prob_ref.shape[0]
    share = own_ref.shape[2]
    half = where_ref[1]
    sums = own_ref[heads] + got_ref[heads]
    for h in range(heads):
        prob = jnp.where(half == 0, prob_ref[h, :, :share], prob_ref[h, :, share:])
        pair_ref[h] = prob * (own_ref[h] + got_ref[h] - sums[:, h : h + 1])
    depth = value_ref.shape[0]
    for t, ref in enumerate((value_ref, gate_ref, output_ref)):
        rows = pl.ds(t * depth, depth)
        ref[...] = totals_ref[rows, :].astype(F32) + more_ref[rows, :].astype(F32)


def call(kernel, outs, spaces, scratch=()):
    spec = {
        "v": pl.BlockSpec(memory_space=pltpu.VMEM),
        "s": pl.BlockSpec(memory_space=pltpu.SMEM),
        "h": pl.BlockSpec(memory_space=pltpu.HBM),
    }
    return pl.pallas_call(
        kernel,
        out_shape=[jax.ShapeDtypeStruct(s, d) for s, d in outs],
        in_specs=[spec[c] for c in spaces],
        out_specs=[spec["v"]] * len(outs),
        scratch_shapes=list(scratch),
        compiler_params=pltpu.CompilerParams(vmem_limit_bytes=48 * 1024 * 1024),
    )


def local_gathered(
    alignment_activations,
    alignment_row_mask,
    residue_mask,
    pair_head_logits,
    value_matrix,
    gate_matrix,
    output_matrix,
    cotangent,
):
    rows, own, depth = alignment_activations.shape
    heads, _, keys = pair_head_logits.shape
    width = value_matrix.shape[1]
    parts = keys // own
    lanes = (2 * rows * depth + heads * keys) // LANES
    where = jnp.stack([lax.axis_index("res"), lax.axis_index("seq")]).astype(jnp.int32)
    packed, prob = call(
        pack_kernel,
        [((lanes * own, LANES), BF16), ((heads, own, keys), F32)],
        "hhhh",
        [
            pltpu.VMEM((rows, own, depth), BF16),
            pltpu.VMEM((rows, own, depth), BF16),
            pltpu.VMEM((heads, own, keys), BF16),
            pltpu.VMEM((1, keys), jnp.int32),
            pltpu.SemaphoreType.DMA((4,)),
        ],
    )(alignment_activations, cotangent, pair_head_logits, residue_mask.reshape(1, keys))

    def swapped(array, bits):
        return lax.ppermute(array, "res", [(i, i ^ bits) for i in range(parts)])

    spread, keep_row, unit, inv = call(
        functools.partial(prepare_kernel, heads),
        [
            ((3, heads // 2, 2 * LANES, 2 * LANES), BF16),
            ((1, rows * width // heads), F32),
            ((rows, own, depth), F32),
            ((rows, own, depth), F32),
        ],
        "svvvv",
    )(alignment_row_mask, alignment_activations, value_matrix, gate_matrix, output_matrix.T)
    line = jnp.concatenate([packed] + [swapped(packed, 4 * k) for k in range(1, parts // 4)])
    plane = jnp.concatenate([line, swapped(line, 2)])
    other = swapped(plane, 1)
    near, far = (a.reshape(parts // 2, lanes, own, LANES) for a in (plane, other))
    share = keys // 2
    align, pair_own, pair_send, totals = call(
        functools.partial(main_kernel, heads),
        [
            ((rows, own, depth), F32),
            ((heads + 1, own, share), F32),
            ((heads + 1, own, share), F32),
            ((3 * depth, width), BF16),
        ],
        "svvvvvvv",
        [pltpu.VMEM((parts, lanes, own, LANES), BF16)]
        + [pltpu.VMEM((heads, keys, 2 * LANES), BF16)] * 3,
    )(where, prob, near, far, spread, keep_row, unit, inv)
    swap = [(0, 1), (1, 0)]
    pair_got = lax.ppermute(pair_send, "seq", swap)
    totals_got = lax.ppermute(totals, "seq", swap)
    pair, value_total, gate_total, output_total = call(
        last_kernel,
        [((heads, own, share), F32)] + [((depth, width), F32)] * 3,
        "svvvvv",
    )(where, prob, pair_own, pair_got, totals, totals_got)
    return align, pair, value_total, gate_total, output_total.T


def fits(mesh, rows, own, depth, heads, keys, width):
    dim = width // heads
    return (
        mesh.shape["seq"] == 2
        and mesh.shape["res"] == 16
        and keys == 2 * LANES
        and own % 16 == 0
        and depth == 2 * dim
        and dim == LANES // 4
        and heads % 4 == 0
        and rows == 8
    )


def layer_standardize(alignment_activations):
    activation_input = alignment_activations.astype(jnp.float32)
    mean_val = jnp.mean(activation_input, axis=-1, keepdims=True)
    centered = activation_input - mean_val
    variance = jnp.mean(centered * centered, axis=-1, keepdims=True)
    inverse_deviation = lax.rsqrt(variance + 1e-05)
    return (centered * inverse_deviation, inverse_deviation)


def gated_back(cot_rows, gate_act, row_keep, output_matrix):
    grad_mixed = lax.dot_general(
        cot_rows, output_matrix, (((2,), (1,)), ((), ())), preferred_element_type=jnp.float32
    )
    return (grad_mixed, (grad_mixed * gate_act * row_keep).astype(jnp.bfloat16))


def block_terms(
    weights, columns, values_all, gate_act, grad_mixed, grad_att, att_all, row_keep, head_count
):
    row_count, key_count, width = values_all.shape
    head_dim = width // head_count
    values_heads = values_all.reshape(row_count, key_count, head_count, head_dim)
    attended = jnp.einsum(
        "hij,sjhc->sihc", weights, values_heads, preferred_element_type=jnp.float32
    )
    attended = attended.reshape(row_count, -1, width)
    mixed_out = (gate_act * attended * row_keep).astype(jnp.bfloat16)
    gate_grad = (grad_mixed * attended * row_keep * gate_act * (1.0 - gate_act)).astype(
        jnp.bfloat16
    )
    att_heads = grad_att.reshape(row_count, -1, head_count, head_dim)
    pair_total = jnp.einsum(
        "sihc,sjhc->hij", att_heads, values_heads, preferred_element_type=jnp.float32
    )
    all_heads = att_all.reshape(row_count, key_count, head_count, head_dim)
    grad_values = jnp.einsum(
        "hij,sihc->sjhc", columns, all_heads, preferred_element_type=jnp.float32
    )
    grad_values = grad_values.reshape(row_count, -1, width).astype(jnp.bfloat16)
    return (pair_total, mixed_out, gate_grad, grad_values)


def local(
    alignment_activations,
    alignment_row_mask,
    residue_mask,
    pair_head_logits,
    value_matrix,
    gate_matrix,
    output_matrix,
    cotangent,
):
    head_count = pair_head_logits.shape[0]
    key_count = pair_head_logits.shape[2]
    unit_alignment, inverse_deviation = layer_standardize(alignment_activations)
    standardized_rows = unit_alignment.astype(jnp.bfloat16)
    key_live = residue_mask == 1
    scores = jnp.where(key_live[None, None, :], pair_head_logits.astype(jnp.float32), -10000.0)
    prob_full = jax.nn.softmax(scores, axis=-1)
    weights = prob_full.astype(jnp.bfloat16)
    columns = lax.all_to_all(weights, "res", split_axis=2, concat_axis=1, tiled=True)
    row_keep = alignment_row_mask.astype(jnp.float32)[:, None, None]
    gate_own = jax.nn.sigmoid(
        jnp.dot(standardized_rows, gate_matrix, preferred_element_type=jnp.float32)
    )
    mixed_own, att_own = gated_back(cotangent, gate_own, row_keep, output_matrix)
    normed_all, cot_all = (
        lax.all_gather(standardized_rows, "res", axis=1, tiled=True),
        lax.all_gather(cotangent, "res", axis=1, tiled=True),
    )
    values_all = jnp.dot(normed_all, value_matrix, preferred_element_type=jnp.float32).astype(
        jnp.bfloat16
    )
    gate_all = jax.nn.sigmoid(jnp.dot(normed_all, gate_matrix, preferred_element_type=jnp.float32))
    mixed_all, att_all = gated_back(cot_all, gate_all, row_keep, output_matrix)
    pair_total, mixed_out, gate_grad, grad_values = block_terms(
        weights, columns, values_all, gate_own, mixed_own, att_own, att_all, row_keep, head_count
    )
    output_weight_gradient = jnp.einsum(
        "sic,sid->cd", mixed_out, cotangent, preferred_element_type=jnp.float32
    )
    value_weight_gradient = jnp.einsum(
        "sic,sid->cd", standardized_rows, grad_values, preferred_element_type=jnp.float32
    )
    gate_weight_gradient = jnp.einsum(
        "sic,sid->cd", standardized_rows, gate_grad, preferred_element_type=jnp.float32
    )
    gradient_totals = lax.psum(
        (value_weight_gradient, gate_weight_gradient, output_weight_gradient), ("res", "seq")
    )
    gradient_standardized = jnp.dot(grad_values, value_matrix.T, preferred_element_type=jnp.float32)
    gradient_standardized = gradient_standardized + jnp.dot(
        gate_grad, gate_matrix.T, preferred_element_type=jnp.float32
    )
    leading_average = jnp.mean(gradient_standardized, axis=-1, keepdims=True)
    trailing_average = jnp.mean(gradient_standardized * unit_alignment, axis=-1, keepdims=True)
    alignment_gradient = inverse_deviation * (
        gradient_standardized - leading_average - unit_alignment * trailing_average
    )
    grad_prob = lax.psum(pair_total, "seq")
    full_grads = prob_full * (grad_prob - jnp.sum(prob_full * grad_prob, axis=-1, keepdims=True))
    share_width = key_count // lax.axis_size("seq")
    pair_logit_gradient = lax.dynamic_slice_in_dim(
        full_grads, lax.axis_index("seq") * share_width, share_width, 2
    )
    return (
        alignment_gradient,
        pair_logit_gradient,
        gradient_totals[0],
        gradient_totals[1],
        gradient_totals[2],
    )


def pick(mesh, *arrays):
    rows, own, depth = arrays[0].shape
    heads, _, keys = arrays[3].shape
    width = arrays[4].shape[1]
    if fits(mesh, rows, own, depth, heads, keys, width):
        return local_gathered(*arrays)
    return local(*arrays)


def solution(mesh):
    return jax.shard_map(
        functools.partial(pick, mesh),
        mesh=mesh,
        in_specs=(
            P(("grp", "seq"), "res", None),
            P(("grp", "seq")),
            P("grp"),
            P(None, ("grp", "res"), None),
            P(),
            P(),
            P(),
            P(("grp", "seq"), "res", None),
        ),
        out_specs=(
            P(("grp", "seq"), "res", None),
            P(None, ("grp", "res"), "seq"),
            P("grp", None),
            P("grp", None),
            P("grp", None),
        ),
        check_vma=False,
    )
```

```python
import functools

import jax
import jax.numpy as jnp
from jax import lax
from jax.experimental import pallas as pl
from jax.experimental.pallas import tpu as pltpu
from jax.sharding import PartitionSpec as P

LANES = 128
F32 = jnp.float32
BF16 = jnp.bfloat16


def dot(a, b):
    return lax.dot_general(a, b, (((1,), (0,)), ((), ())), preferred_element_type=F32)


def dot_nt(a, b):
    return lax.dot_general(a, b, (((1,), (1,)), ((), ())), preferred_element_type=F32)


def dot_tn(a, b):
    return lax.dot_general(a, b, (((0,), (0,)), ((), ())), preferred_element_type=F32)


def standardize(x):
    x = x.astype(F32)
    centered = x - jnp.mean(x, axis=-1, keepdims=True)
    inv = lax.rsqrt(jnp.mean(centered * centered, axis=-1, keepdims=True) + 1e-05)
    return centered * inv, inv


def fetch(sources, targets, sems):
    copies = [
        pltpu.make_async_copy(src, dst, sems.at[i])
        for i, (src, dst) in enumerate(zip(sources, targets))
    ]
    for copy in copies:
        copy.start()
    return copies


def pack_kernel(
    acts_hbm, cot_hbm, logits_hbm, live_hbm, rows_ref, weights_ref, prob_ref,
    acts_ref, cot_ref, logits_ref, live_ref, sems,
):
    copies = fetch(
        (acts_hbm, cot_hbm, logits_hbm, live_hbm), (acts_ref, cot_ref, logits_ref, live_ref), sems
    )
    rows, own, depth = acts_ref.shape
    heads, _, keys = logits_ref.shape
    per = LANES // depth
    blocks = rows // per
    wide = keys // LANES
    copies[0].wait()
    unit, _ = standardize(acts_ref[...])
    normed = unit.astype(BF16)
    for b in range(blocks):
        rows_ref[pl.ds(b * own, own), :] = jnp.concatenate(
            [normed[b * per + k] for k in range(per)], axis=-1
        )
    copies[1].wait()
    cot = cot_ref[...]
    for b in range(blocks):
        rows_ref[pl.ds((blocks + b) * own, own), :] = jnp.concatenate(
            [cot[b * per + k] for k in range(per)], axis=-1
        )
    copies[2].wait()
    copies[3].wait()
    live = live_ref[...] == 1
    for h in range(heads):
        scores = jnp.where(live, logits_ref[h].astype(F32), -10000.0)
        e = jnp.exp(scores - jnp.max(scores, axis=-1, keepdims=True))
        prob = e / jnp.sum(e, axis=-1, keepdims=True)
        prob_ref[h] = prob
        weights = prob.astype(BF16)
        for w in range(wide):
            weights_ref[pl.ds((h * wide + w) * own, own), :] = weights[
                :, w * LANES : (w + 1) * LANES
            ]


def prepare_kernel(
    heads,
    keep_ref,
    acts_ref,
    value_ref,
    gate_ref,
    output_ref,
    spread_ref,
    keep_row_ref,
    unit_ref,
    inv_ref,
):
    rows, _, depth = acts_ref.shape
    width = value_ref.shape[1]
    dim = width // heads
    quad = LANES // dim
    slot = lax.broadcasted_iota(jnp.int32, (1, LANES), 1) // dim
    for g in range(rows // quad):
        row = jnp.zeros((1, LANES), F32)
        for k in range(quad):
            row = jnp.where(slot == k, keep_ref[g * quad + k].astype(F32), row)
        keep_row_ref[:, g * LANES : (g + 1) * LANES] = row
    src = lax.broadcasted_iota(jnp.int32, (width, 2 * LANES), 0)
    dst = lax.broadcasted_iota(jnp.int32, (width, 2 * LANES), 1)
    spread_to = (dst // LANES) * dim + dst % dim
    mask_row = lax.broadcasted_iota(jnp.int32, (quad * depth, 2 * LANES), 0) // depth
    mask_col = (lax.broadcasted_iota(jnp.int32, (quad * depth, 2 * LANES), 1) % LANES) // dim
    diagonal = mask_row == mask_col
    for p in range(heads // 2):
        spread = (src == spread_to + 2 * p * dim).astype(BF16)
        for t, ref in enumerate((value_ref, gate_ref, output_ref)):
            tall = jnp.concatenate([dot(ref[...], spread)] * quad, axis=0)
            spread_ref[t, p] = jnp.where(diagonal, tall, 0.0).astype(BF16)
    unit, inv = standardize(acts_ref[...])
    unit_ref[...] = unit
    inv_ref[...] = jnp.broadcast_to(inv, unit.shape)


def main_kernel(
    heads,
    where_ref,
    prob_ref,
    near_rows_ref,
    far_rows_ref,
    near_weights_ref,
    far_weights_ref,
    spread_ref,
    keep_row_ref,
    own_grad_ref,
    pair_own_ref,
    send_ref,
    rows_ref,
    weights_ref,
    att_ref,
    val_grad_ref,
    gate_grad_ref,
):
    parts, blocks, own, _ = rows_ref.shape
    blocks = blocks // 2
    keys = parts * own
    share = keys // 2
    depth = LANES // 2
    quad = spread_ref.shape[2] // depth
    dim = LANES // quad
    groups = keep_row_ref.shape[1] // LANES
    width = heads * dim
    span = blocks // groups
    wide = keys // LANES
    first = pl.multiple_of(where_ref[0] * own, own)
    half = where_ref[1]
    for r in range(parts):
        away = where_ref[0] ^ r
        side, column, level = away % 2, away // 2 % 2, away // 4
        spot = level * 2 + column
        rows_ref[r] = jnp.where(side == 0, near_rows_ref[spot], far_rows_ref[spot])
        spot = column * (parts // 4) + level
        weights_ref[r] = jnp.where(side == 0, near_weights_ref[spot], far_weights_ref[spot])

    def row_block(start):
        return jnp.concatenate(
            [rows_ref[:, start + k].reshape(keys, LANES) for k in range(span)], axis=1
        )

    x = [row_block(g * span) for g in range(groups)]
    y = [row_block(blocks + g * span) for g in range(groups)]
    x_t = [a.T for a in x]
    y_t = [a.T for a in y]

    lane = lax.broadcasted_iota(jnp.int32, (1, LANES), 1)
    slot = lane // dim
    keep_row = keep_row_ref[...]
    fold_slot = (lax.broadcasted_iota(jnp.int32, (depth, 2 * LANES), 1) % LANES) // dim

    def fold(total):
        picked = total[:depth]
        for k in range(1, quad):
            picked = jnp.where(fold_slot == k, total[k * depth : (k + 1) * depth], picked)
        out = []
        for h in range(2):
            part = picked[:, h * LANES : (h + 1) * LANES]
            step = LANES // 2
            while step >= dim:
                part = part + pltpu.roll(part, step, 1)
                step //= 2
            out.append(part)
        return out

    def put_pair(h, pair):
        top = pair.astype(BF16)
        at = 3 * depth * (width // LANES) + h * own
        send_ref[pl.ds(at, own), :] = top
        send_ref[pl.ds(at + (heads + 1) * own, own), :] = (pair - top.astype(F32)).astype(BF16)

    folded = [[], [], []]
    sums = jnp.zeros((own, LANES), F32)
    for p in range(heads // 2):
        value_bd = spread_ref[0, p]
        gate_bd = spread_ref[1, p]
        output_bd = spread_ref[2, p]
        values = [dot(a, value_bd).astype(BF16) for a in x]
        gates = [dot(a, gate_bd) for a in x]
        mixes = [dot(a, output_bd) for a in y]
        mixed_out, gate_grad, val_grad = [], [], []
        for k in range(2):
            h = 2 * p + k
            cut = slice(k * LANES, (k + 1) * LANES)
            weights = jnp.concatenate(
                [weights_ref[:, h * wide + w].reshape(keys, LANES) for w in range(wide)], axis=1
            )
            vals = jnp.concatenate([v[:, cut] for v in values], axis=1)
            attended = dot(weights, vals)
            gate = jax.nn.sigmoid(jnp.concatenate([v[:, cut] for v in gates], axis=1))
            mixed = jnp.concatenate([v[:, cut] for v in mixes], axis=1)
            kept = gate * keep_row
            grad_att = mixed * kept
            att_bf = grad_att.astype(BF16)
            att_ref[h] = att_bf
            mixed_out.append((kept * attended).astype(BF16))
            gate_grad.append((grad_att * attended * (1.0 - gate)).astype(BF16))
            val_grad.append(dot_tn(weights, att_bf).astype(BF16))
            pair = dot_nt(att_ref[h, pl.ds(first, own), :], vals)
            prob = prob_ref[h]
            sums = jnp.where(lane == h, jnp.sum(prob * pair, axis=-1, keepdims=True), sums)
            low, high = pair[:, : keys // 2], pair[:, keys // 2 :]
            pair_own_ref[h] = jnp.where(half == 0, low, high)
            put_pair(h, jnp.where(half == 0, high, low))
        totals = [None, None, None]
        for g in range(groups):
            cut = slice(g * LANES, (g + 1) * LANES)
            mo = jnp.concatenate([a[:, cut] for a in mixed_out], axis=1)
            gg = jnp.concatenate([a[:, cut] for a in gate_grad], axis=1)
            vg = jnp.concatenate([a[:, cut] for a in val_grad], axis=1)
            gate_grad_ref[p * groups + g] = gg
            val_grad_ref[p * groups + g] = vg
            own_grad_ref[0, p * groups + g] = val_grad_ref[p * groups + g, pl.ds(first, own), :]
            own_grad_ref[1, p * groups + g] = gate_grad_ref[p * groups + g, pl.ds(first, own), :]
            for t, (left, right) in enumerate(((x_t, vg), (x_t, gg), (y_t, mo))):
                term = dot(left[g], right)
                totals[t] = term if totals[t] is None else totals[t] + term
        for t in range(3):
            folded[t].extend(fold(totals[t]))

    put_pair(heads, sums)
    pair_own_ref[heads] = sums
    for t in range(3):
        for b in range(width // LANES):
            block = folded[t][b * quad]
            for k in range(1, quad):
                block = jnp.where(slot == k, folded[t][b * quad + k], block)
            at = (t * (width // LANES) + b) * depth
            send_ref[pl.ds(at, depth), :] = block.astype(BF16)


def align_kernel(spread_ref, unit_ref, inv_ref, own_grad_ref, align_ref):
    rows, own, depth = unit_ref.shape
    pairs = spread_ref.shape[1]
    groups = own_grad_ref.shape[1] // pairs
    quad = rows // groups
    for g in range(groups):
        total = jnp.zeros((own, quad * depth), F32)
        for p in range(pairs):
            for t in range(2):
                total = total + dot_nt(own_grad_ref[t, p * groups + g], spread_ref[t, p])
        for k in range(quad):
            s = g * quad + k
            grad = total[:, k * depth : (k + 1) * depth]
            lead = jnp.mean(grad, axis=-1, keepdims=True)
            trail = jnp.mean(grad * unit_ref[s], axis=-1, keepdims=True)
            align_ref[s] = inv_ref[s] * (grad - lead - unit_ref[s] * trail)


def last_kernel(
    where_ref, prob_ref, own_ref, mine_ref, got_ref, pair_ref, value_ref, gate_ref, output_ref
):
    heads, own, keys = prob_ref.shape
    share = keys // 2
    depth, width = value_ref.shape
    half = where_ref[1]

    def got_pair(h):
        at = 3 * depth * (width // LANES) + h * own
        top = got_ref[pl.ds(at, own), :].astype(F32)
        return top + got_ref[pl.ds(at + (heads + 1) * own, own), :].astype(F32)

    sums = own_ref[heads] + got_pair(heads)
    for h in range(heads):
        prob = jnp.where(half == 0, prob_ref[h, :, :share], prob_ref[h, :, share:])
        pair_ref[h] = prob * (own_ref[h] + got_pair(h) - sums[:, h : h + 1])
    for t, ref in enumerate((value_ref, gate_ref, output_ref)):
        for b in range(width // LANES):
            at = pl.ds((t * (width // LANES) + b) * depth, depth)
            ref[:, b * LANES : (b + 1) * LANES] = mine_ref[at, :].astype(F32) + got_ref[
                at, :
            ].astype(F32)


def call(kernel, outs, spaces, scratch=(), limit=16 * 1024 * 1024, cost=None):
    spec = {
        "v": pl.BlockSpec(memory_space=pltpu.VMEM),
        "s": pl.BlockSpec(memory_space=pltpu.SMEM),
        "h": pl.BlockSpec(memory_space=pltpu.HBM),
    }
    return pl.pallas_call(
        kernel,
        out_shape=[jax.ShapeDtypeStruct(s, d) for s, d in outs],
        in_specs=[spec[c] for c in spaces],
        out_specs=[spec["v"]] * len(outs),
        scratch_shapes=list(scratch),
        compiler_params=pltpu.CompilerParams(vmem_limit_bytes=limit),
        cost_estimate=cost,
    )


def local_gathered(
    alignment_activations,
    alignment_row_mask,
    residue_mask,
    pair_head_logits,
    value_matrix,
    gate_matrix,
    output_matrix,
    cotangent,
):
    rows, own, depth = alignment_activations.shape
    heads, _, keys = pair_head_logits.shape
    width = value_matrix.shape[1]
    parts = keys // own
    row_blocks = 2 * rows * depth // LANES
    weight_blocks = heads * keys // LANES
    share = keys // 2
    where = jnp.stack([lax.axis_index("res"), lax.axis_index("seq")]).astype(jnp.int32)
    packed_rows, packed_weights, prob = call(
        pack_kernel,
        [
            ((row_blocks * own, LANES), BF16),
            ((weight_blocks * own, LANES), BF16),
            ((heads, own, keys), F32),
        ],
        "hhhh",
        [
            pltpu.VMEM((rows, own, depth), BF16),
            pltpu.VMEM((rows, own, depth), BF16),
            pltpu.VMEM((heads, own, keys), BF16),
            pltpu.VMEM((1, keys), jnp.int32),
            pltpu.SemaphoreType.DMA((4,)),
        ],
        None,
    )(alignment_activations, cotangent, pair_head_logits, residue_mask.reshape(1, keys))

    def swapped(array, bits):
        return lax.ppermute(array, "res", [(i, i ^ bits) for i in range(parts)])

    def line(array):
        return jnp.concatenate([array] + [swapped(array, 4 * k) for k in range(1, parts // 4)])

    spread, keep_row, unit, inv = call(
        functools.partial(prepare_kernel, heads),
        [
            ((3, heads // 2, 2 * LANES, 2 * LANES), BF16),
            ((1, rows * width // heads), F32),
            ((rows, own, depth), F32),
            ((rows, own, depth), F32),
        ],
        "svvvv",
    )(alignment_row_mask, alignment_activations, value_matrix, gate_matrix, output_matrix.T)
    weights_line = line(packed_weights)
    rows_pair = jnp.concatenate([packed_rows, swapped(packed_rows, 2)])
    weights_plane = jnp.concatenate([weights_line, swapped(weights_line, 2)])
    rows_plane = line(rows_pair)

    def split(array, blocks):
        return array.reshape(parts // 2, blocks, own, LANES)

    own_grad, pair_own, send = call(
        functools.partial(main_kernel, heads),
        [
            ((2, heads // 2 * rows * width // heads // LANES, own, 2 * LANES), BF16),
            ((heads + 1, own, share), F32),
            ((3 * depth * width // LANES + 2 * (heads + 1) * own, LANES), BF16),
        ],
        "svvvvvvv",
        [
            pltpu.VMEM((parts, row_blocks, own, LANES), BF16),
            pltpu.VMEM((parts, weight_blocks, own, LANES), BF16),
        ]
        + [pltpu.VMEM((heads, keys, 2 * LANES), BF16)] * 3,
        32 * 1024 * 1024,
    )(
        where,
        prob,
        split(rows_plane, row_blocks),
        split(swapped(rows_plane, 1), row_blocks),
        split(weights_plane, weight_blocks),
        split(swapped(weights_plane, 1), weight_blocks),
        spread,
        keep_row,
    )
    got = lax.ppermute(send, "seq", [(0, 1), (1, 0)])
    (align,) = call(align_kernel, [((rows, own, depth), F32)], "vvvv")(
        spread, unit, inv, own_grad
    )
    pair, value_total, gate_total, output_total = call(
        last_kernel,
        [((heads, own, share), F32)] + [((depth, width), F32)] * 3,
        "svvvv",
    )(where, prob, pair_own, send, got)
    return align, pair, value_total, gate_total, output_total.T


def fits(mesh, rows, own, depth, heads, keys, width):
    dim = width // heads
    return (
        mesh.shape["seq"] == 2
        and mesh.shape["res"] == 16
        and keys == 2 * LANES
        and own % 16 == 0
        and depth == 2 * dim
        and dim == LANES // 4
        and heads % 4 == 0
        and rows == 8
    )


def layer_standardize(alignment_activations):
    activation_input = alignment_activations.astype(jnp.float32)
    mean_val = jnp.mean(activation_input, axis=-1, keepdims=True)
    centered = activation_input - mean_val
    variance = jnp.mean(centered * centered, axis=-1, keepdims=True)
    inverse_deviation = lax.rsqrt(variance + 1e-05)
    return (centered * inverse_deviation, inverse_deviation)


def gated_back(cot_rows, gate_act, row_keep, output_matrix):
    grad_mixed = lax.dot_general(
        cot_rows, output_matrix, (((2,), (1,)), ((), ())), preferred_element_type=jnp.float32
    )
    return (grad_mixed, (grad_mixed * gate_act * row_keep).astype(jnp.bfloat16))


def block_terms(
    weights, columns, values_all, gate_act, grad_mixed, grad_att, att_all, row_keep, head_count
):
    row_count, key_count, width = values_all.shape
    head_dim = width // head_count
    values_heads = values_all.reshape(row_count, key_count, head_count, head_dim)
    attended = jnp.einsum(
        "hij,sjhc->sihc", weights, values_heads, preferred_element_type=jnp.float32
    )
    attended = attended.reshape(row_count, -1, width)
    mixed_out = (gate_act * attended * row_keep).astype(jnp.bfloat16)
    gate_grad = (grad_mixed * attended * row_keep * gate_act * (1.0 - gate_act)).astype(
        jnp.bfloat16
    )
    att_heads = grad_att.reshape(row_count, -1, head_count, head_dim)
    pair_total = jnp.einsum(
        "sihc,sjhc->hij", att_heads, values_heads, preferred_element_type=jnp.float32
    )
    all_heads = att_all.reshape(row_count, key_count, head_count, head_dim)
    grad_values = jnp.einsum(
        "hij,sihc->sjhc", columns, all_heads, preferred_element_type=jnp.float32
    )
    grad_values = grad_values.reshape(row_count, -1, width).astype(jnp.bfloat16)
    return (pair_total, mixed_out, gate_grad, grad_values)


def local(
    alignment_activations,
    alignment_row_mask,
    residue_mask,
    pair_head_logits,
    value_matrix,
    gate_matrix,
    output_matrix,
    cotangent,
):
    head_count = pair_head_logits.shape[0]
    key_count = pair_head_logits.shape[2]
    unit_alignment, inverse_deviation = layer_standardize(alignment_activations)
    standardized_rows = unit_alignment.astype(jnp.bfloat16)
    key_live = residue_mask == 1
    scores = jnp.where(key_live[None, None, :], pair_head_logits.astype(jnp.float32), -10000.0)
    prob_full = jax.nn.softmax(scores, axis=-1)
    weights = prob_full.astype(jnp.bfloat16)
    columns = lax.all_to_all(weights, "res", split_axis=2, concat_axis=1, tiled=True)
    row_keep = alignment_row_mask.astype(jnp.float32)[:, None, None]
    gate_own = jax.nn.sigmoid(
        jnp.dot(standardized_rows, gate_matrix, preferred_element_type=jnp.float32)
    )
    mixed_own, att_own = gated_back(cotangent, gate_own, row_keep, output_matrix)
    normed_all, cot_all = (
        lax.all_gather(standardized_rows, "res", axis=1, tiled=True),
        lax.all_gather(cotangent, "res", axis=1, tiled=True),
    )
    values_all = jnp.dot(normed_all, value_matrix, preferred_element_type=jnp.float32).astype(
        jnp.bfloat16
    )
    gate_all = jax.nn.sigmoid(jnp.dot(normed_all, gate_matrix, preferred_element_type=jnp.float32))
    mixed_all, att_all = gated_back(cot_all, gate_all, row_keep, output_matrix)
    pair_total, mixed_out, gate_grad, grad_values = block_terms(
        weights, columns, values_all, gate_own, mixed_own, att_own, att_all, row_keep, head_count
    )
    output_weight_gradient = jnp.einsum(
        "sic,sid->cd", mixed_out, cotangent, preferred_element_type=jnp.float32
    )
    value_weight_gradient = jnp.einsum(
        "sic,sid->cd", standardized_rows, grad_values, preferred_element_type=jnp.float32
    )
    gate_weight_gradient = jnp.einsum(
        "sic,sid->cd", standardized_rows, gate_grad, preferred_element_type=jnp.float32
    )
    gradient_totals = lax.psum(
        (value_weight_gradient, gate_weight_gradient, output_weight_gradient), ("res", "seq")
    )
    gradient_standardized = jnp.dot(grad_values, value_matrix.T, preferred_element_type=jnp.float32)
    gradient_standardized = gradient_standardized + jnp.dot(
        gate_grad, gate_matrix.T, preferred_element_type=jnp.float32
    )
    leading_average = jnp.mean(gradient_standardized, axis=-1, keepdims=True)
    trailing_average = jnp.mean(gradient_standardized * unit_alignment, axis=-1, keepdims=True)
    alignment_gradient = inverse_deviation * (
        gradient_standardized - leading_average - unit_alignment * trailing_average
    )
    grad_prob = lax.psum(pair_total, "seq")
    full_grads = prob_full * (grad_prob - jnp.sum(prob_full * grad_prob, axis=-1, keepdims=True))
    share_width = key_count // lax.axis_size("seq")
    pair_logit_gradient = lax.dynamic_slice_in_dim(
        full_grads, lax.axis_index("seq") * share_width, share_width, 2
    )
    return (
        alignment_gradient,
        pair_logit_gradient,
        gradient_totals[0],
        gradient_totals[1],
        gradient_totals[2],
    )


def pick(mesh, *arrays):
    rows, own, depth = arrays[0].shape
    heads, _, keys = arrays[3].shape
    width = arrays[4].shape[1]
    if fits(mesh, rows, own, depth, heads, keys, width):
        return local_gathered(*arrays)
    return local(*arrays)


def solution(mesh):
    return jax.shard_map(
        functools.partial(pick, mesh),
        mesh=mesh,
        in_specs=(
            P(("grp", "seq"), "res", None),
            P(("grp", "seq")),
            P("grp"),
            P(None, ("grp", "res"), None),
            P(),
            P(),
            P(),
            P(("grp", "seq"), "res", None),
        ),
        out_specs=(
            P(("grp", "seq"), "res", None),
            P(None, ("grp", "res"), "seq"),
            P("grp", None),
            P("grp", None),
            P("grp", None),
        ),
        check_vma=False,
    )
```

```python
import functools

import jax
import jax.numpy as jnp
from jax import lax
from jax.experimental import pallas as pl
from jax.experimental.pallas import tpu as pltpu
from jax.sharding import PartitionSpec as P

LANES = 128
F32 = jnp.float32
BF16 = jnp.bfloat16


def dot(a, b):
    return lax.dot_general(a, b, (((1,), (0,)), ((), ())), preferred_element_type=F32)


def dot_nt(a, b):
    return lax.dot_general(a, b, (((1,), (1,)), ((), ())), preferred_element_type=F32)


def dot_tn(a, b):
    return lax.dot_general(a, b, (((0,), (0,)), ((), ())), preferred_element_type=F32)


def standardize(x):
    x = x.astype(F32)
    centered = x - jnp.mean(x, axis=-1, keepdims=True)
    inv = lax.rsqrt(jnp.mean(centered * centered, axis=-1, keepdims=True) + 1e-05)
    return centered * inv, inv


def fetch(sources, targets, sems):
    copies = [
        pltpu.make_async_copy(src, dst, sems.at[i])
        for i, (src, dst) in enumerate(zip(sources, targets))
    ]
    for copy in copies:
        copy.start()
    return copies


def pack_kernel(
    acts_hbm, cot_hbm, logits_hbm, live_hbm, both_ref, prob_ref,
    acts_ref, cot_ref, logits_ref, live_ref, sems,
):
    copies = fetch(
        (acts_hbm, cot_hbm, logits_hbm, live_hbm), (acts_ref, cot_ref, logits_ref, live_ref), sems
    )
    rows, own, depth = acts_ref.shape
    heads, _, keys = logits_ref.shape
    per = LANES // depth
    blocks = rows // per
    wide = keys // LANES
    head_blocks = heads * wide
    copies[0].wait()
    unit, _ = standardize(acts_ref[...])
    normed = unit.astype(BF16)
    for b in range(blocks):
        both_ref[pl.ds((head_blocks + b) * own, own), :] = jnp.concatenate(
            [normed[b * per + k] for k in range(per)], axis=-1
        )
    copies[1].wait()
    cot = cot_ref[...]
    for b in range(blocks):
        both_ref[pl.ds((head_blocks + blocks + b) * own, own), :] = jnp.concatenate(
            [cot[b * per + k] for k in range(per)], axis=-1
        )
    copies[2].wait()
    copies[3].wait()
    live = live_ref[...] == 1
    for h in range(heads):
        scores = jnp.where(live, logits_ref[h].astype(F32), -10000.0)
        e = jnp.exp(scores - jnp.max(scores, axis=-1, keepdims=True))
        prob = e / jnp.sum(e, axis=-1, keepdims=True)
        prob_ref[h] = prob
        weights = prob.astype(BF16)
        for w in range(wide):
            block = weights[:, w * LANES : (w + 1) * LANES]
            both_ref[pl.ds((h * wide + w) * own, own), :] = block


def prepare_kernel(
    heads,
    keep_ref,
    acts_ref,
    value_ref,
    gate_ref,
    output_ref,
    spread_ref,
    keep_row_ref,
    unit_ref,
    inv_ref,
):
    rows, _, depth = acts_ref.shape
    width = value_ref.shape[1]
    dim = width // heads
    quad = LANES // dim
    slot = lax.broadcasted_iota(jnp.int32, (1, LANES), 1) // dim
    for g in range(rows // quad):
        row = jnp.zeros((1, LANES), F32)
        for k in range(quad):
            row = jnp.where(slot == k, keep_ref[g * quad + k].astype(F32), row)
        keep_row_ref[:, g * LANES : (g + 1) * LANES] = row
    src = lax.broadcasted_iota(jnp.int32, (width, 2 * LANES), 0)
    dst = lax.broadcasted_iota(jnp.int32, (width, 2 * LANES), 1)
    spread_to = (dst // LANES) * dim + dst % dim
    mask_row = lax.broadcasted_iota(jnp.int32, (quad * depth, 2 * LANES), 0) // depth
    mask_col = (lax.broadcasted_iota(jnp.int32, (quad * depth, 2 * LANES), 1) % LANES) // dim
    diagonal = mask_row == mask_col
    for p in range(heads // 2):
        spread = (src == spread_to + 2 * p * dim).astype(BF16)
        for t, ref in enumerate((value_ref, gate_ref, output_ref)):
            tall = jnp.concatenate([dot(ref[...], spread)] * quad, axis=0)
            spread_ref[t, p] = jnp.where(diagonal, tall, 0.0).astype(BF16)
    unit, inv = standardize(acts_ref[...])
    unit_ref[...] = unit
    inv_ref[...] = jnp.broadcast_to(inv, unit.shape)


def place(me, first, count, near_ref, near_beside_ref, far_ref, far_beside_ref, out_ref):
    parts = out_ref.shape[0]
    cut = pl.ds(first, count)
    sources = (near_ref, far_ref, near_beside_ref, far_beside_ref)
    for low in range(4):

        @pl.when(me % 4 == low)
        def _():
            for r in range(parts):
                level = me // 4 ^ r // 4
                out_ref[r] = sources[low ^ r % 4][level % 2 * 2 + level // 2, cut]


def main_kernel(
    heads,
    where_ref,
    prob_ref,
    near_ref,
    near_late_ref,
    far_ref,
    far_late_ref,
    spread_ref,
    keep_row_ref,
    own_grad_ref,
    pair_own_ref,
    send_ref,
    rows_ref,
    weights_ref,
    att_ref,
    val_grad_ref,
    gate_grad_ref,
):
    parts, blocks, own, _ = rows_ref.shape
    blocks = blocks // 2
    keys = parts * own
    share = keys // 2
    depth = LANES // 2
    quad = spread_ref.shape[2] // depth
    dim = LANES // quad
    groups = keep_row_ref.shape[1] // LANES
    width = heads * dim
    span = blocks // groups
    wide = keys // LANES
    first = pl.multiple_of(where_ref[0] * own, own)
    half = where_ref[1]
    sources = (near_ref, near_late_ref, far_ref, far_late_ref)
    place(where_ref[0], weights_ref.shape[1], 2 * blocks, *sources, rows_ref)
    place(where_ref[0], 0, weights_ref.shape[1], *sources, weights_ref)

    def row_block(start):
        return jnp.concatenate(
            [rows_ref[:, start + k].reshape(keys, LANES) for k in range(span)], axis=1
        )

    x = [row_block(g * span) for g in range(groups)]
    y = [row_block(blocks + g * span) for g in range(groups)]
    x_t = [a.T for a in x]
    y_t = [a.T for a in y]

    lane = lax.broadcasted_iota(jnp.int32, (1, LANES), 1)
    slot = lane // dim
    keep_row = keep_row_ref[...]
    fold_slot = (lax.broadcasted_iota(jnp.int32, (depth, 2 * LANES), 1) % LANES) // dim

    def fold(total):
        picked = total[:depth]
        for k in range(1, quad):
            picked = jnp.where(fold_slot == k, total[k * depth : (k + 1) * depth], picked)
        out = []
        for h in range(2):
            part = picked[:, h * LANES : (h + 1) * LANES]
            step = LANES // 2
            while step >= dim:
                part = part + pltpu.roll(part, step, 1)
                step //= 2
            out.append(part)
        return out

    def put_pair(h, pair):
        top = pair.astype(BF16)
        at = 3 * depth * (width // LANES) + h * own
        send_ref[pl.ds(at, own), :] = top
        send_ref[pl.ds(at + (heads + 1) * own, own), :] = (pair - top.astype(F32)).astype(BF16)

    folded = [[], [], []]
    sums = jnp.zeros((own, LANES), F32)
    for p in range(heads // 2):
        value_bd = spread_ref[0, p]
        gate_bd = spread_ref[1, p]
        output_bd = spread_ref[2, p]
        values = [dot(a, value_bd).astype(BF16) for a in x]
        gates = [dot(a, gate_bd) for a in x]
        mixes = [dot(a, output_bd) for a in y]
        mixed_out, gate_grad, val_grad = [], [], []
        for k in range(2):
            h = 2 * p + k
            cut = slice(k * LANES, (k + 1) * LANES)
            weights = jnp.concatenate(
                [weights_ref[:, h * wide + w].reshape(keys, LANES) for w in range(wide)], axis=1
            )
            vals = jnp.concatenate([v[:, cut] for v in values], axis=1)
            attended = dot(weights, vals)
            gate = jax.nn.sigmoid(jnp.concatenate([v[:, cut] for v in gates], axis=1))
            mixed = jnp.concatenate([v[:, cut] for v in mixes], axis=1)
            kept = gate * keep_row
            grad_att = mixed * kept
            att_bf = grad_att.astype(BF16)
            att_ref[h] = att_bf
            mixed_out.append((kept * attended).astype(BF16))
            gate_grad.append((grad_att * attended * (1.0 - gate)).astype(BF16))
            val_grad.append(dot_tn(weights, att_bf).astype(BF16))
            pair = dot_nt(att_ref[h, pl.ds(first, own), :], vals)
            prob = prob_ref[h]
            sums = jnp.where(lane == h, jnp.sum(prob * pair, axis=-1, keepdims=True), sums)
            low, high = pair[:, : keys // 2], pair[:, keys // 2 :]
            pair_own_ref[h] = jnp.where(half == 0, low, high)
            put_pair(h, jnp.where(half == 0, high, low))
        totals = [None, None, None]
        for g in range(groups):
            cut = slice(g * LANES, (g + 1) * LANES)
            mo = jnp.concatenate([a[:, cut] for a in mixed_out], axis=1)
            gg = jnp.concatenate([a[:, cut] for a in gate_grad], axis=1)
            vg = jnp.concatenate([a[:, cut] for a in val_grad], axis=1)
            gate_grad_ref[p * groups + g] = gg
            val_grad_ref[p * groups + g] = vg
            own_grad_ref[0, p * groups + g] = val_grad_ref[p * groups + g, pl.ds(first, own), :]
            own_grad_ref[1, p * groups + g] = gate_grad_ref[p * groups + g, pl.ds(first, own), :]
            for t, (left, right) in enumerate(((x_t, vg), (x_t, gg), (y_t, mo))):
                term = dot(left[g], right)
                totals[t] = term if totals[t] is None else totals[t] + term
        for t in range(3):
            folded[t].extend(fold(totals[t]))

    put_pair(heads, sums)
    pair_own_ref[heads] = sums
    for t in range(3):
        for b in range(width // LANES):
            block = folded[t][b * quad]
            for k in range(1, quad):
                block = jnp.where(slot == k, folded[t][b * quad + k], block)
            at = (t * (width // LANES) + b) * depth
            send_ref[pl.ds(at, depth), :] = block.astype(BF16)


def align_kernel(spread_ref, unit_ref, inv_ref, own_grad_ref, align_ref):
    rows, own, depth = unit_ref.shape
    pairs = spread_ref.shape[1]
    groups = own_grad_ref.shape[1] // pairs
    quad = rows // groups
    for g in range(groups):
        total = jnp.zeros((own, quad * depth), F32)
        for p in range(pairs):
            for t in range(2):
                total = total + dot_nt(own_grad_ref[t, p * groups + g], spread_ref[t, p])
        for k in range(quad):
            s = g * quad + k
            grad = total[:, k * depth : (k + 1) * depth]
            lead = jnp.mean(grad, axis=-1, keepdims=True)
            trail = jnp.mean(grad * unit_ref[s], axis=-1, keepdims=True)
            align_ref[s] = inv_ref[s] * (grad - lead - unit_ref[s] * trail)


def last_kernel(
    where_ref, prob_ref, own_ref, mine_ref, got_ref, pair_ref, value_ref, gate_ref, output_ref
):
    heads, own, keys = prob_ref.shape
    share = keys // 2
    depth, width = value_ref.shape
    half = where_ref[1]

    def got_pair(h):
        at = 3 * depth * (width // LANES) + h * own
        top = got_ref[pl.ds(at, own), :].astype(F32)
        return top + got_ref[pl.ds(at + (heads + 1) * own, own), :].astype(F32)

    sums = own_ref[heads] + got_pair(heads)
    for h in range(heads):
        prob = jnp.where(half == 0, prob_ref[h, :, :share], prob_ref[h, :, share:])
        pair_ref[h] = prob * (own_ref[h] + got_pair(h) - sums[:, h : h + 1])
    for t, ref in enumerate((value_ref, gate_ref, output_ref)):
        for b in range(width // LANES):
            at = pl.ds((t * (width // LANES) + b) * depth, depth)
            ref[:, b * LANES : (b + 1) * LANES] = mine_ref[at, :].astype(F32) + got_ref[
                at, :
            ].astype(F32)


def call(kernel, outs, spaces, scratch=(), limit=16 * 1024 * 1024, cost=0):
    spec = {
        "v": pl.BlockSpec(memory_space=pltpu.VMEM),
        "s": pl.BlockSpec(memory_space=pltpu.SMEM),
        "h": pl.BlockSpec(memory_space=pltpu.HBM),
    }
    return pl.pallas_call(
        kernel,
        out_shape=[jax.ShapeDtypeStruct(s, d) for s, d in outs],
        in_specs=[spec[c] for c in spaces],
        out_specs=[spec["v"]] * len(outs),
        scratch_shapes=list(scratch),
        compiler_params=pltpu.CompilerParams(vmem_limit_bytes=limit),
        cost_estimate=pl.CostEstimate(
            flops=cost * 1150000000, bytes_accessed=0, transcendentals=0
        ),
    )


def local_gathered(
    alignment_activations,
    alignment_row_mask,
    residue_mask,
    pair_head_logits,
    value_matrix,
    gate_matrix,
    output_matrix,
    cotangent,
):
    rows, own, depth = alignment_activations.shape
    heads, _, keys = pair_head_logits.shape
    width = value_matrix.shape[1]
    parts = keys // own
    row_blocks = 2 * rows * depth // LANES
    weight_blocks = heads * keys // LANES
    share = keys // 2
    where = jnp.stack([lax.axis_index("res"), lax.axis_index("seq")]).astype(jnp.int32)
    both, prob = call(
        pack_kernel,
        [
            (((row_blocks + weight_blocks) * own, LANES), BF16),
            ((heads, own, keys), F32),
        ],
        "hhhh",
        [
            pltpu.VMEM((rows, own, depth), BF16),
            pltpu.VMEM((rows, own, depth), BF16),
            pltpu.VMEM((heads, own, keys), BF16),
            pltpu.VMEM((1, keys), jnp.int32),
            pltpu.SemaphoreType.DMA((4,)),
        ],
        None,
    )(alignment_activations, cotangent, pair_head_logits, residue_mask.reshape(1, keys))

    def swapped(array, bits):
        return lax.ppermute(array, "res", [(i, i ^ bits) for i in range(parts)])

    spread, keep_row, unit, inv = call(
        functools.partial(prepare_kernel, heads),
        [
            ((3, heads // 2, 2 * LANES, 2 * LANES), BF16),
            ((1, rows * width // heads), F32),
            ((rows, own, depth), F32),
            ((rows, own, depth), F32),
        ],
        "svvvv",
        cost=1,
    )(alignment_row_mask, alignment_activations, value_matrix, gate_matrix, output_matrix.T)
    level_2 = swapped(both, 8)
    level_1 = swapped(both, 4)
    beside = swapped(both, 2)
    level_3 = swapped(level_2, 4)
    beside_2 = swapped(level_2, 2)
    beside_13 = swapped(jnp.concatenate([level_1, level_3]), 2)
    early = jnp.concatenate([both, level_2, level_1, level_3])
    late = jnp.concatenate([beside, beside_2, beside_13])

    def split(array):
        return array.reshape(-1, row_blocks + weight_blocks, own, LANES)

    own_grad, pair_own, send = call(
        functools.partial(main_kernel, heads),
        [
            ((2, heads // 2 * rows * width // heads // LANES, own, 2 * LANES), BF16),
            ((heads + 1, own, share), F32),
            ((3 * depth * width // LANES + 2 * (heads + 1) * own, LANES), BF16),
        ],
        "svvvvvvv",
        [
            pltpu.VMEM((parts, row_blocks, own, LANES), BF16),
            pltpu.VMEM((parts, weight_blocks, own, LANES), BF16),
        ]
        + [pltpu.VMEM((heads, keys, 2 * LANES), BF16)] * 3,
        32 * 1024 * 1024,
        cost=5,
    )(
        where,
        prob,
        split(early),
        split(late),
        split(swapped(early, 1)),
        split(swapped(late, 1)),
        spread,
        keep_row,
    )
    got = lax.ppermute(send, "seq", [(0, 1), (1, 0)])
    (align,) = call(align_kernel, [((rows, own, depth), F32)], "vvvv", cost=2)(
        spread, unit, inv, own_grad
    )
    pair, value_total, gate_total, output_total = call(
        last_kernel,
        [((heads, own, share), F32)] + [((depth, width), F32)] * 3,
        "svvvv",
    )(where, prob, pair_own, send, got)
    return align, pair, value_total, gate_total, output_total.T


def fits(mesh, rows, own, depth, heads, keys, width):
    dim = width // heads
    return (
        mesh.shape["seq"] == 2
        and mesh.shape["res"] == 16
        and keys == 2 * LANES
        and own % 16 == 0
        and depth == 2 * dim
        and dim == LANES // 4
        and heads % 4 == 0
        and rows == 8
    )


def layer_standardize(alignment_activations):
    activation_input = alignment_activations.astype(jnp.float32)
    mean_val = jnp.mean(activation_input, axis=-1, keepdims=True)
    centered = activation_input - mean_val
    variance = jnp.mean(centered * centered, axis=-1, keepdims=True)
    inverse_deviation = lax.rsqrt(variance + 1e-05)
    return (centered * inverse_deviation, inverse_deviation)


def gated_back(cot_rows, gate_act, row_keep, output_matrix):
    grad_mixed = lax.dot_general(
        cot_rows, output_matrix, (((2,), (1,)), ((), ())), preferred_element_type=jnp.float32
    )
    return (grad_mixed, (grad_mixed * gate_act * row_keep).astype(jnp.bfloat16))


def block_terms(
    weights, columns, values_all, gate_act, grad_mixed, grad_att, att_all, row_keep, head_count
):
    row_count, key_count, width = values_all.shape
    head_dim = width // head_count
    values_heads = values_all.reshape(row_count, key_count, head_count, head_dim)
    attended = jnp.einsum(
        "hij,sjhc->sihc", weights, values_heads, preferred_element_type=jnp.float32
    )
    attended = attended.reshape(row_count, -1, width)
    mixed_out = (gate_act * attended * row_keep).astype(jnp.bfloat16)
    gate_grad = (grad_mixed * attended * row_keep * gate_act * (1.0 - gate_act)).astype(
        jnp.bfloat16
    )
    att_heads = grad_att.reshape(row_count, -1, head_count, head_dim)
    pair_total = jnp.einsum(
        "sihc,sjhc->hij", att_heads, values_heads, preferred_element_type=jnp.float32
    )
    all_heads = att_all.reshape(row_count, key_count, head_count, head_dim)
    grad_values = jnp.einsum(
        "hij,sihc->sjhc", columns, all_heads, preferred_element_type=jnp.float32
    )
    grad_values = grad_values.reshape(row_count, -1, width).astype(jnp.bfloat16)
    return (pair_total, mixed_out, gate_grad, grad_values)


def local(
    alignment_activations,
    alignment_row_mask,
    residue_mask,
    pair_head_logits,
    value_matrix,
    gate_matrix,
    output_matrix,
    cotangent,
):
    head_count = pair_head_logits.shape[0]
    key_count = pair_head_logits.shape[2]
    unit_alignment, inverse_deviation = layer_standardize(alignment_activations)
    standardized_rows = unit_alignment.astype(jnp.bfloat16)
    key_live = residue_mask == 1
    scores = jnp.where(key_live[None, None, :], pair_head_logits.astype(jnp.float32), -10000.0)
    prob_full = jax.nn.softmax(scores, axis=-1)
    weights = prob_full.astype(jnp.bfloat16)
    columns = lax.all_to_all(weights, "res", split_axis=2, concat_axis=1, tiled=True)
    row_keep = alignment_row_mask.astype(jnp.float32)[:, None, None]
    gate_own = jax.nn.sigmoid(
        jnp.dot(standardized_rows, gate_matrix, preferred_element_type=jnp.float32)
    )
    mixed_own, att_own = gated_back(cotangent, gate_own, row_keep, output_matrix)
    normed_all, cot_all = (
        lax.all_gather(standardized_rows, "res", axis=1, tiled=True),
        lax.all_gather(cotangent, "res", axis=1, tiled=True),
    )
    values_all = jnp.dot(normed_all, value_matrix, preferred_element_type=jnp.float32).astype(
        jnp.bfloat16
    )
    gate_all = jax.nn.sigmoid(jnp.dot(normed_all, gate_matrix, preferred_element_type=jnp.float32))
    mixed_all, att_all = gated_back(cot_all, gate_all, row_keep, output_matrix)
    pair_total, mixed_out, gate_grad, grad_values = block_terms(
        weights, columns, values_all, gate_own, mixed_own, att_own, att_all, row_keep, head_count
    )
    output_weight_gradient = jnp.einsum(
        "sic,sid->cd", mixed_out, cotangent, preferred_element_type=jnp.float32
    )
    value_weight_gradient = jnp.einsum(
        "sic,sid->cd", standardized_rows, grad_values, preferred_element_type=jnp.float32
    )
    gate_weight_gradient = jnp.einsum(
        "sic,sid->cd", standardized_rows, gate_grad, preferred_element_type=jnp.float32
    )
    gradient_totals = lax.psum(
        (value_weight_gradient, gate_weight_gradient, output_weight_gradient), ("res", "seq")
    )
    gradient_standardized = jnp.dot(grad_values, value_matrix.T, preferred_element_type=jnp.float32)
    gradient_standardized = gradient_standardized + jnp.dot(
        gate_grad, gate_matrix.T, preferred_element_type=jnp.float32
    )
    leading_average = jnp.mean(gradient_standardized, axis=-1, keepdims=True)
    trailing_average = jnp.mean(gradient_standardized * unit_alignment, axis=-1, keepdims=True)
    alignment_gradient = inverse_deviation * (
        gradient_standardized - leading_average - unit_alignment * trailing_average
    )
    grad_prob = lax.psum(pair_total, "seq")
    full_grads = prob_full * (grad_prob - jnp.sum(prob_full * grad_prob, axis=-1, keepdims=True))
    share_width = key_count // lax.axis_size("seq")
    pair_logit_gradient = lax.dynamic_slice_in_dim(
        full_grads, lax.axis_index("seq") * share_width, share_width, 2
    )
    return (
        alignment_gradient,
        pair_logit_gradient,
        gradient_totals[0],
        gradient_totals[1],
        gradient_totals[2],
    )


def pick(mesh, *arrays):
    rows, own, depth = arrays[0].shape
    heads, _, keys = arrays[3].shape
    width = arrays[4].shape[1]
    if fits(mesh, rows, own, depth, heads, keys, width):
        return local_gathered(*arrays)
    return local(*arrays)


def solution(mesh):
    return jax.shard_map(
        functools.partial(pick, mesh),
        mesh=mesh,
        in_specs=(
            P(("grp", "seq"), "res", None),
            P(("grp", "seq")),
            P("grp"),
            P(None, ("grp", "res"), None),
            P(),
            P(),
            P(),
            P(("grp", "seq"), "res", None),
        ),
        out_specs=(
            P(("grp", "seq"), "res", None),
            P(None, ("grp", "res"), "seq"),
            P("grp", None),
            P("grp", None),
            P("grp", None),
        ),
        check_vma=False,
    )
```

```python
import functools

import jax
import jax.numpy as jnp
from jax import lax
from jax.experimental import pallas as pl
from jax.experimental.pallas import tpu as pltpu
from jax.sharding import PartitionSpec as P

LANES = 128
F32 = jnp.float32
BF16 = jnp.bfloat16


def dot(a, b):
    return lax.dot_general(a, b, (((1,), (0,)), ((), ())), preferred_element_type=F32)


def dot_nt(a, b):
    return lax.dot_general(a, b, (((1,), (1,)), ((), ())), preferred_element_type=F32)


def dot_tn(a, b):
    return lax.dot_general(a, b, (((0,), (0,)), ((), ())), preferred_element_type=F32)


def standardize(x):
    x = x.astype(F32)
    centered = x - jnp.mean(x, axis=-1, keepdims=True)
    inv = lax.rsqrt(jnp.mean(centered * centered, axis=-1, keepdims=True) + 1e-05)
    return centered * inv, inv


def fetch(sources, targets, sems):
    copies = [
        pltpu.make_async_copy(src, dst, sems.at[i])
        for i, (src, dst) in enumerate(zip(sources, targets))
    ]
    for copy in copies:
        copy.start()
    return copies


def pack_kernel(
    acts_hbm, cot_hbm, logits_hbm, live_hbm, both_ref, prob_ref,
    acts_ref, cot_ref, logits_ref, live_ref, sems,
):
    copies = fetch(
        (acts_hbm, cot_hbm, logits_hbm, live_hbm), (acts_ref, cot_ref, logits_ref, live_ref), sems
    )
    rows, own, depth = acts_ref.shape
    heads, _, keys = logits_ref.shape
    per = LANES // depth
    blocks = rows // per
    wide = keys // LANES
    head_blocks = heads * wide
    copies[0].wait()
    unit, _ = standardize(acts_ref[...])
    normed = unit.astype(BF16)
    for b in range(blocks):
        both_ref[pl.ds((head_blocks + b) * own, own), :] = jnp.concatenate(
            [normed[b * per + k] for k in range(per)], axis=-1
        )
    copies[1].wait()
    cot = cot_ref[...]
    for b in range(blocks):
        both_ref[pl.ds((head_blocks + blocks + b) * own, own), :] = jnp.concatenate(
            [cot[b * per + k] for k in range(per)], axis=-1
        )
    copies[2].wait()
    copies[3].wait()
    live = live_ref[...] == 1
    for h in range(heads):
        scores = jnp.where(live, logits_ref[h].astype(F32), -10000.0)
        e = jnp.exp(scores - jnp.max(scores, axis=-1, keepdims=True))
        prob = e / jnp.sum(e, axis=-1, keepdims=True)
        prob_ref[h] = prob
        weights = prob.astype(BF16)
        for w in range(wide):
            block = weights[:, w * LANES : (w + 1) * LANES]
            both_ref[pl.ds((h * wide + w) * own, own), :] = block


def prepare_kernel(
    heads,
    keep_ref,
    acts_ref,
    value_ref,
    gate_ref,
    output_ref,
    spread_ref,
    keep_row_ref,
    unit_ref,
    inv_ref,
):
    rows, _, depth = acts_ref.shape
    width = value_ref.shape[1]
    dim = width // heads
    quad = LANES // dim
    slot = lax.broadcasted_iota(jnp.int32, (1, LANES), 1) // dim
    for g in range(rows // quad):
        row = jnp.zeros((1, LANES), F32)
        for k in range(quad):
            row = jnp.where(slot == k, keep_ref[g * quad + k].astype(F32), row)
        keep_row_ref[:, g * LANES : (g + 1) * LANES] = row
    src = lax.broadcasted_iota(jnp.int32, (width, 2 * LANES), 0)
    dst = lax.broadcasted_iota(jnp.int32, (width, 2 * LANES), 1)
    spread_to = (dst // LANES) * dim + dst % dim
    mask_row = lax.broadcasted_iota(jnp.int32, (quad * depth, 2 * LANES), 0) // depth
    mask_col = (lax.broadcasted_iota(jnp.int32, (quad * depth, 2 * LANES), 1) % LANES) // dim
    diagonal = mask_row == mask_col
    for p in range(heads // 2):
        spread = (src == spread_to + 2 * p * dim).astype(BF16)
        for t, ref in enumerate((value_ref, gate_ref, output_ref)):
            tall = jnp.concatenate([dot(ref[...], spread)] * quad, axis=0)
            spread_ref[t, p] = jnp.where(diagonal, tall, 0.0).astype(BF16)
    unit, inv = standardize(acts_ref[...])
    unit_ref[...] = unit
    inv_ref[...] = jnp.broadcast_to(inv, unit.shape)


def place(me, first, count, near_ref, near_beside_ref, far_ref, far_beside_ref, out_ref):
    parts = out_ref.shape[0]
    cut = pl.ds(first, count)
    sources = (near_ref, far_ref, near_beside_ref, far_beside_ref)
    for low in range(4):

        @pl.when(me % 4 == low)
        def _():
            for r in range(parts):
                level = me // 4 ^ r // 4
                out_ref[r] = sources[low ^ r % 4][level % 2 * 2 + level // 2, cut]


def main_kernel(
    heads,
    where_ref,
    prob_ref,
    near_ref,
    near_late_ref,
    far_ref,
    far_late_ref,
    spread_ref,
    keep_row_ref,
    own_grad_ref,
    pair_own_ref,
    send_ref,
    rows_ref,
    weights_ref,
    att_ref,
    val_grad_ref,
    gate_grad_ref,
):
    parts, blocks, own, _ = rows_ref.shape
    blocks = blocks // 2
    keys = parts * own
    share = keys // 2
    depth = LANES // 2
    quad = spread_ref.shape[2] // depth
    dim = LANES // quad
    groups = keep_row_ref.shape[1] // LANES
    width = heads * dim
    span = blocks // groups
    wide = keys // LANES
    first = pl.multiple_of(where_ref[0] * own, own)
    half = where_ref[1]
    sources = (near_ref, near_late_ref, far_ref, far_late_ref)
    place(where_ref[0], weights_ref.shape[1], 2 * blocks, *sources, rows_ref)
    place(where_ref[0], 0, weights_ref.shape[1], *sources, weights_ref)

    def row_block(start):
        return jnp.concatenate(
            [rows_ref[:, start + k].reshape(keys, LANES) for k in range(span)], axis=1
        )

    x = [row_block(g * span) for g in range(groups)]
    y = [row_block(blocks + g * span) for g in range(groups)]
    x_t = jnp.concatenate([a.T for a in x], axis=1)
    y_t = jnp.concatenate([a.T for a in y], axis=1)

    lane = lax.broadcasted_iota(jnp.int32, (1, LANES), 1)
    slot = lane // dim
    keep_row = keep_row_ref[...]
    fold_slot = (lax.broadcasted_iota(jnp.int32, (depth, 2 * LANES), 1) % LANES) // dim

    def fold(total):
        picked = total[:depth]
        for k in range(1, quad):
            picked = jnp.where(fold_slot == k, total[k * depth : (k + 1) * depth], picked)
        out = []
        for h in range(2):
            part = picked[:, h * LANES : (h + 1) * LANES]
            step = LANES // 2
            while step >= dim:
                part = part + pltpu.roll(part, step, 1)
                step //= 2
            out.append(part)
        return out

    def put_pair(h, pair):
        top = pair.astype(BF16)
        at = 3 * depth * (width // LANES) + h * own
        send_ref[pl.ds(at, own), :] = top
        send_ref[pl.ds(at + (heads + 1) * own, own), :] = (pair - top.astype(F32)).astype(BF16)

    folded = [[], [], []]
    sums = jnp.zeros((own, LANES), F32)
    for p in range(heads // 2):
        value_bd = spread_ref[0, p]
        gate_bd = spread_ref[1, p]
        output_bd = spread_ref[2, p]
        values = [dot(a, value_bd).astype(BF16) for a in x]
        gates = [dot(a, gate_bd) for a in x]
        mixes = [dot(a, output_bd) for a in y]
        mixed_out, gate_grad, val_grad = [], [], []
        for k in range(2):
            h = 2 * p + k
            cut = slice(k * LANES, (k + 1) * LANES)
            weights = jnp.concatenate(
                [weights_ref[:, h * wide + w].reshape(keys, LANES) for w in range(wide)], axis=1
            )
            vals = jnp.concatenate([v[:, cut] for v in values], axis=1)
            attended = dot(weights, vals)
            gate = 0.5 + 0.5 * jnp.tanh(0.5 * jnp.concatenate([v[:, cut] for v in gates], axis=1))
            mixed = jnp.concatenate([v[:, cut] for v in mixes], axis=1)
            kept = gate * keep_row
            grad_att = mixed * kept
            att_bf = grad_att.astype(BF16)
            att_ref[h] = att_bf
            mixed_out.append((kept * attended).astype(BF16))
            gate_grad.append((grad_att * attended * (1.0 - gate)).astype(BF16))
            val_grad.append(dot_tn(weights, att_bf).astype(BF16))
            pair = dot_nt(att_ref[h, pl.ds(first, own), :], vals)
            prob = prob_ref[h]
            sums = jnp.where(lane == h, jnp.sum(prob * pair, axis=-1, keepdims=True), sums)
            low, high = pair[:, : keys // 2], pair[:, keys // 2 :]
            pair_own_ref[h] = jnp.where(half == 0, low, high)
            put_pair(h, jnp.where(half == 0, high, low))
        parts_of = [[], [], []]
        for g in range(groups):
            cut = slice(g * LANES, (g + 1) * LANES)
            mo = jnp.concatenate([a[:, cut] for a in mixed_out], axis=1)
            gg = jnp.concatenate([a[:, cut] for a in gate_grad], axis=1)
            vg = jnp.concatenate([a[:, cut] for a in val_grad], axis=1)
            gate_grad_ref[p * groups + g] = gg
            val_grad_ref[p * groups + g] = vg
            own_grad_ref[0, p * groups + g] = val_grad_ref[p * groups + g, pl.ds(first, own), :]
            own_grad_ref[1, p * groups + g] = gate_grad_ref[p * groups + g, pl.ds(first, own), :]
            for t, part in enumerate((vg, gg, mo)):
                parts_of[t].append(part)
        totals = [
            dot(left, jnp.concatenate(parts_of[t], axis=0))
            for t, left in enumerate((x_t, x_t, y_t))
        ]
        for t in range(3):
            folded[t].extend(fold(totals[t]))

    put_pair(heads, sums)
    pair_own_ref[heads] = sums
    for t in range(3):
        for b in range(width // LANES):
            block = folded[t][b * quad]
            for k in range(1, quad):
                block = jnp.where(slot == k, folded[t][b * quad + k], block)
            at = (t * (width // LANES) + b) * depth
            send_ref[pl.ds(at, depth), :] = block.astype(BF16)


def align_kernel(spread_ref, unit_ref, inv_ref, own_grad_ref, align_ref):
    rows, own, depth = unit_ref.shape
    pairs = spread_ref.shape[1]
    groups = own_grad_ref.shape[1] // pairs
    quad = rows // groups
    for g in range(groups):
        total = jnp.zeros((own, quad * depth), F32)
        for p in range(pairs):
            for t in range(2):
                total = total + dot_nt(own_grad_ref[t, p * groups + g], spread_ref[t, p])
        for k in range(quad):
            s = g * quad + k
            grad = total[:, k * depth : (k + 1) * depth]
            lead = jnp.mean(grad, axis=-1, keepdims=True)
            trail = jnp.mean(grad * unit_ref[s], axis=-1, keepdims=True)
            align_ref[s] = inv_ref[s] * (grad - lead - unit_ref[s] * trail)


def last_kernel(
    where_ref, prob_ref, own_ref, mine_ref, got_ref, pair_ref, value_ref, gate_ref, output_ref
):
    heads, own, keys = prob_ref.shape
    share = keys // 2
    depth, width = value_ref.shape
    half = where_ref[1]

    def got_pair(h):
        at = 3 * depth * (width // LANES) + h * own
        top = got_ref[pl.ds(at, own), :].astype(F32)
        return top + got_ref[pl.ds(at + (heads + 1) * own, own), :].astype(F32)

    sums = own_ref[heads] + got_pair(heads)
    for h in range(heads):
        prob = jnp.where(half == 0, prob_ref[h, :, :share], prob_ref[h, :, share:])
        pair_ref[h] = prob * (own_ref[h] + got_pair(h) - sums[:, h : h + 1])
    for t, ref in enumerate((value_ref, gate_ref, output_ref)):
        for b in range(width // LANES):
            at = pl.ds((t * (width // LANES) + b) * depth, depth)
            ref[:, b * LANES : (b + 1) * LANES] = mine_ref[at, :].astype(F32) + got_ref[
                at, :
            ].astype(F32)


def call(kernel, outs, spaces, scratch=(), limit=16 * 1024 * 1024, cost=0):
    spec = {
        "v": pl.BlockSpec(memory_space=pltpu.VMEM),
        "s": pl.BlockSpec(memory_space=pltpu.SMEM),
        "h": pl.BlockSpec(memory_space=pltpu.HBM),
    }
    return pl.pallas_call(
        kernel,
        out_shape=[jax.ShapeDtypeStruct(s, d) for s, d in outs],
        in_specs=[spec[c] for c in spaces],
        out_specs=[spec["v"]] * len(outs),
        scratch_shapes=list(scratch),
        compiler_params=pltpu.CompilerParams(vmem_limit_bytes=limit),
        cost_estimate=pl.CostEstimate(
            flops=cost * 1150000000, bytes_accessed=0, transcendentals=0
        ),
    )


def local_gathered(
    alignment_activations,
    alignment_row_mask,
    residue_mask,
    pair_head_logits,
    value_matrix,
    gate_matrix,
    output_matrix,
    cotangent,
):
    rows, own, depth = alignment_activations.shape
    heads, _, keys = pair_head_logits.shape
    width = value_matrix.shape[1]
    parts = keys // own
    row_blocks = 2 * rows * depth // LANES
    weight_blocks = heads * keys // LANES
    share = keys // 2
    where = jnp.stack([lax.axis_index("res"), lax.axis_index("seq")]).astype(jnp.int32)
    both, prob = call(
        pack_kernel,
        [
            (((row_blocks + weight_blocks) * own, LANES), BF16),
            ((heads, own, keys), F32),
        ],
        "hhhh",
        [
            pltpu.VMEM((rows, own, depth), BF16),
            pltpu.VMEM((rows, own, depth), BF16),
            pltpu.VMEM((heads, own, keys), BF16),
            pltpu.VMEM((1, keys), jnp.int32),
            pltpu.SemaphoreType.DMA((4,)),
        ],
        None,
    )(alignment_activations, cotangent, pair_head_logits, residue_mask.reshape(1, keys))

    def swapped(array, bits):
        return lax.ppermute(array, "res", [(i, i ^ bits) for i in range(parts)])

    spread, keep_row, unit, inv = call(
        functools.partial(prepare_kernel, heads),
        [
            ((3, heads // 2, 2 * LANES, 2 * LANES), BF16),
            ((1, rows * width // heads), F32),
            ((rows, own, depth), F32),
            ((rows, own, depth), F32),
        ],
        "svvvv",
        cost=1,
    )(alignment_row_mask, alignment_activations, value_matrix, gate_matrix, output_matrix.T)
    level_2 = swapped(both, 8)
    level_1 = swapped(both, 4)
    beside = swapped(both, 2)
    level_3 = swapped(level_2, 4)
    beside_2 = swapped(level_2, 2)
    beside_1 = swapped(level_1, 2)
    beside_3 = swapped(level_3, 2)
    early = jnp.concatenate([both, level_2, level_1, level_3])
    late = jnp.concatenate([beside, beside_2, beside_1, beside_3])

    def split(array):
        return array.reshape(-1, row_blocks + weight_blocks, own, LANES)

    own_grad, pair_own, send = call(
        functools.partial(main_kernel, heads),
        [
            ((2, heads // 2 * rows * width // heads // LANES, own, 2 * LANES), BF16),
            ((heads + 1, own, share), F32),
            ((3 * depth * width // LANES + 2 * (heads + 1) * own, LANES), BF16),
        ],
        "svvvvvvv",
        [
            pltpu.VMEM((parts, row_blocks, own, LANES), BF16),
            pltpu.VMEM((parts, weight_blocks, own, LANES), BF16),
        ]
        + [pltpu.VMEM((heads, keys, 2 * LANES), BF16)] * 3,
        32 * 1024 * 1024,
        cost=5,
    )(
        where,
        prob,
        split(early),
        split(late),
        split(swapped(early, 1)),
        split(swapped(late, 1)),
        spread,
        keep_row,
    )
    got = lax.ppermute(send, "seq", [(0, 1), (1, 0)])
    (align,) = call(align_kernel, [((rows, own, depth), F32)], "vvvv", cost=2)(
        spread, unit, inv, own_grad
    )
    pair, value_total, gate_total, output_total = call(
        last_kernel,
        [((heads, own, share), F32)] + [((depth, width), F32)] * 3,
        "svvvv",
    )(where, prob, pair_own, send, got)
    return align, pair, value_total, gate_total, output_total.T


def fits(mesh, rows, own, depth, heads, keys, width):
    dim = width // heads
    return (
        mesh.shape["seq"] == 2
        and mesh.shape["res"] == 16
        and keys == 2 * LANES
        and own % 16 == 0
        and depth == 2 * dim
        and dim == LANES // 4
        and heads % 4 == 0
        and rows == 8
    )


def layer_standardize(alignment_activations):
    activation_input = alignment_activations.astype(jnp.float32)
    mean_val = jnp.mean(activation_input, axis=-1, keepdims=True)
    centered = activation_input - mean_val
    variance = jnp.mean(centered * centered, axis=-1, keepdims=True)
    inverse_deviation = lax.rsqrt(variance + 1e-05)
    return (centered * inverse_deviation, inverse_deviation)


def gated_back(cot_rows, gate_act, row_keep, output_matrix):
    grad_mixed = lax.dot_general(
        cot_rows, output_matrix, (((2,), (1,)), ((), ())), preferred_element_type=jnp.float32
    )
    return (grad_mixed, (grad_mixed * gate_act * row_keep).astype(jnp.bfloat16))


def block_terms(
    weights, columns, values_all, gate_act, grad_mixed, grad_att, att_all, row_keep, head_count
):
    row_count, key_count, width = values_all.shape
    head_dim = width // head_count
    values_heads = values_all.reshape(row_count, key_count, head_count, head_dim)
    attended = jnp.einsum(
        "hij,sjhc->sihc", weights, values_heads, preferred_element_type=jnp.float32
    )
    attended = attended.reshape(row_count, -1, width)
    mixed_out = (gate_act * attended * row_keep).astype(jnp.bfloat16)
    gate_grad = (grad_mixed * attended * row_keep * gate_act * (1.0 - gate_act)).astype(
        jnp.bfloat16
    )
    att_heads = grad_att.reshape(row_count, -1, head_count, head_dim)
    pair_total = jnp.einsum(
        "sihc,sjhc->hij", att_heads, values_heads, preferred_element_type=jnp.float32
    )
    all_heads = att_all.reshape(row_count, key_count, head_count, head_dim)
    grad_values = jnp.einsum(
        "hij,sihc->sjhc", columns, all_heads, preferred_element_type=jnp.float32
    )
    grad_values = grad_values.reshape(row_count, -1, width).astype(jnp.bfloat16)
    return (pair_total, mixed_out, gate_grad, grad_values)


def local(
    alignment_activations,
    alignment_row_mask,
    residue_mask,
    pair_head_logits,
    value_matrix,
    gate_matrix,
    output_matrix,
    cotangent,
):
    head_count = pair_head_logits.shape[0]
    key_count = pair_head_logits.shape[2]
    unit_alignment, inverse_deviation = layer_standardize(alignment_activations)
    standardized_rows = unit_alignment.astype(jnp.bfloat16)
    key_live = residue_mask == 1
    scores = jnp.where(key_live[None, None, :], pair_head_logits.astype(jnp.float32), -10000.0)
    prob_full = jax.nn.softmax(scores, axis=-1)
    weights = prob_full.astype(jnp.bfloat16)
    columns = lax.all_to_all(weights, "res", split_axis=2, concat_axis=1, tiled=True)
    row_keep = alignment_row_mask.astype(jnp.float32)[:, None, None]
    gate_own = jax.nn.sigmoid(
        jnp.dot(standardized_rows, gate_matrix, preferred_element_type=jnp.float32)
    )
    mixed_own, att_own = gated_back(cotangent, gate_own, row_keep, output_matrix)
    normed_all, cot_all = (
        lax.all_gather(standardized_rows, "res", axis=1, tiled=True),
        lax.all_gather(cotangent, "res", axis=1, tiled=True),
    )
    values_all = jnp.dot(normed_all, value_matrix, preferred_element_type=jnp.float32).astype(
        jnp.bfloat16
    )
    gate_all = jax.nn.sigmoid(jnp.dot(normed_all, gate_matrix, preferred_element_type=jnp.float32))
    mixed_all, att_all = gated_back(cot_all, gate_all, row_keep, output_matrix)
    pair_total, mixed_out, gate_grad, grad_values = block_terms(
        weights, columns, values_all, gate_own, mixed_own, att_own, att_all, row_keep, head_count
    )
    output_weight_gradient = jnp.einsum(
        "sic,sid->cd", mixed_out, cotangent, preferred_element_type=jnp.float32
    )
    value_weight_gradient = jnp.einsum(
        "sic,sid->cd", standardized_rows, grad_values, preferred_element_type=jnp.float32
    )
    gate_weight_gradient = jnp.einsum(
        "sic,sid->cd", standardized_rows, gate_grad, preferred_element_type=jnp.float32
    )
    gradient_totals = lax.psum(
        (value_weight_gradient, gate_weight_gradient, output_weight_gradient), ("res", "seq")
    )
    gradient_standardized = jnp.dot(grad_values, value_matrix.T, preferred_element_type=jnp.float32)
    gradient_standardized = gradient_standardized + jnp.dot(
        gate_grad, gate_matrix.T, preferred_element_type=jnp.float32
    )
    leading_average = jnp.mean(gradient_standardized, axis=-1, keepdims=True)
    trailing_average = jnp.mean(gradient_standardized * unit_alignment, axis=-1, keepdims=True)
    alignment_gradient = inverse_deviation * (
        gradient_standardized - leading_average - unit_alignment * trailing_average
    )
    grad_prob = lax.psum(pair_total, "seq")
    full_grads = prob_full * (grad_prob - jnp.sum(prob_full * grad_prob, axis=-1, keepdims=True))
    share_width = key_count // lax.axis_size("seq")
    pair_logit_gradient = lax.dynamic_slice_in_dim(
        full_grads, lax.axis_index("seq") * share_width, share_width, 2
    )
    return (
        alignment_gradient,
        pair_logit_gradient,
        gradient_totals[0],
        gradient_totals[1],
        gradient_totals[2],
    )


def pick(mesh, *arrays):
    rows, own, depth = arrays[0].shape
    heads, _, keys = arrays[3].shape
    width = arrays[4].shape[1]
    if fits(mesh, rows, own, depth, heads, keys, width):
        return local_gathered(*arrays)
    return local(*arrays)


def solution(mesh):
    return jax.shard_map(
        functools.partial(pick, mesh),
        mesh=mesh,
        in_specs=(
            P(("grp", "seq"), "res", None),
            P(("grp", "seq")),
            P("grp"),
            P(None, ("grp", "res"), None),
            P(),
            P(),
            P(),
            P(("grp", "seq"), "res", None),
        ),
        out_specs=(
            P(("grp", "seq"), "res", None),
            P(None, ("grp", "res"), "seq"),
            P("grp", None),
            P("grp", None),
            P("grp", None),
        ),
        check_vma=False,
    )
```
